256 devices in a mesh: rows: 64 (over z, y, core), dims: 4 (over x).
Axes of the slice: x: 4, y: 4, z: 8, core: 2. Of those that a mesh axis runs over, the one named last changes fastest.
Arguments:
- table: bfloat16 [1, 256, 262144], P(None, 'dims', 'rows'), may hold values from -6 to 6
- accum: float32 [1, 262144], P(None, 'rows'), may hold values from 0.5 to 8
- grad_pooled: bfloat16 [1, 256, 8192], P(None, 'dims', 'rows'), may hold values from -6 to 6
- sample_slot: int32 [1, 64, 64, 160], P(None, 'rows'), may hold values from 0 to 127
- row_slot: int32 [1, 64, 64, 160], P(None, 'rows'), may hold values from 0 to 4095
- weight: int32 [1, 64, 64, 160], P(None, 'rows'), may hold values from 1 to 3
- send_count: int32 [1, 64, 64], P(None, 'rows'), may hold values from 1 to 160, as said below
Outputs:
- pooled: float32 [1, 256, 8192], P(None, 'dims', 'rows')
- new_table: bfloat16 [1, 256, 262144], P(None, 'dims', 'rows')
- new_accum: float32 [1, 262144], P(None, 'rows')
The draws below stay inside these ranges and needn't reach their ends.
Inputs may be any that keep to these rules, and one draw needn't show every extreme that they name: `send_count`: at most 160 live entries from one row shard to one owner per feature; in every feature one owner receives exactly 160 from every row shard. Slots at or after the count are unused.
All inputs are finite; a program needn't handle non-finite values.
Results may differ from the reference program's by a relative error of at most 0.001.
Values may be sent and summed in bfloat16 or wider, within the bound.
A program may use at most 64 MiB of HBM per device.

```python
import math
import jax
import jax.numpy as jnp
import numpy as np
from jax import lax

D = 256
FEAT = 1
LR = 4096
SPD = 128
CAP = 160
ROWS = 262144
SAMPLES = 8192
N_ROWS = 64


def draw_send_count(key, part):
    base_key, full_key = jax.random.split(jax.random.fold_in(key, 17))
    base_count = jax.random.randint(base_key, (FEAT, N_ROWS, N_ROWS), 1, CAP + 1)
    full_owner = jax.random.randint(full_key, (FEAT, 1, 1), 0, N_ROWS)
    owner_index = lax.broadcasted_iota(jnp.int32, (FEAT, N_ROWS, N_ROWS), 2)
    return jnp.where(owner_index == full_owner, CAP, base_count).astype(jnp.int32)


def plant(drawn, own_key, least, high):
    dims = drawn.shape
    place = [jax.random.randint(jax.random.fold_in(own_key, axis), (), 0, dims[axis]) for axis in range(len(dims))]
    drawn = drawn.at[tuple(place)].set(least)
    longest = dims.index(max(dims))
    place[longest] = (place[longest] + 1) % dims[longest]
    return drawn.at[tuple(place)].set(high)


def level_of(key, shape, shards, least, largest):
    def one(position, parts):
        heights = jax.random.uniform(jax.random.fold_in(jax.random.fold_in(key, 6), position), (parts,), jnp.float32, least / len(shards), largest / len(shards))
        return jnp.repeat(jnp.exp(heights), shape[position] // parts).reshape((-1,) + (1,) * (len(shape) - position - 1))

    loudness = one(*shards[0])
    for cut in shards[1:]:
        loudness = loudness * one(*cut)
    return loudness


def rank_table(number_of, slope):
    loads = [(1 << 20) // math.isqrt(standing ** slope) + 1 for standing in range(1, number_of + 1)]
    spread = 1 + sum(loads) // (1 << 30)
    return np.cumsum(np.array([max(1, weight // spread) for weight in loads]))


def ranked_ids(rng, shape, amount, skew):
    table = rank_table(amount, skew)
    ticket = jax.random.randint(jax.random.fold_in(rng, 1), shape, 0, int(table[amount - 1]))
    rank = jnp.searchsorted(jnp.asarray(table, jnp.int32), ticket, side="right")
    return jax.random.permutation(jax.random.fold_in(rng, 2), amount)[rank].astype(jnp.int32)


def centred(rng, dims, width, reach, cuts=(), kind=jnp.bfloat16):
    entries = jax.random.normal(rng, dims, jnp.float32) * width
    if len(cuts) > 0:
        entries = level_of(rng, dims, cuts, -0.22, 0.18) * entries
    return jnp.clip(entries, min=-reach, max=reach).astype(kind)


def setup_inputs(seed: int = 0) -> dict:
    key_list = jax.random.split(jax.random.key(seed), 8)
    return {
        "table": centred(key_list[0], (FEAT, D, ROWS), 1.0, 6.0, ((1, 4), (2, 64))),
        "accum": jnp.clip(jnp.exp(math.log(8.0) - 2.7725887 * jax.random.uniform(key_list[1], (FEAT, ROWS), jnp.float32) ** level_of(key_list[1], (FEAT, ROWS), ((1, 64),), -0.2, 0.2)), 0.5, 8.0),
        "grad_pooled": centred(key_list[2], (FEAT, D, SAMPLES), 1.0, 6.0, ((1, 4), (2, 64))),
        "sample_slot": plant(jax.random.randint(key_list[3], (FEAT, N_ROWS, N_ROWS, CAP), 0, SPD), jax.random.fold_in(key_list[3], 1), 0, SPD - 1).astype(jnp.int32),
        "row_slot": plant(ranked_ids(key_list[4], (FEAT, N_ROWS, N_ROWS, CAP), LR, 2), jax.random.fold_in(key_list[4], 3), 0, LR - 1).astype(jnp.int32),
        "weight": plant(jax.random.randint(key_list[5], (FEAT, N_ROWS, N_ROWS, CAP), 1, 4), jax.random.fold_in(key_list[5], 1), 1, 3).astype(jnp.int32),
        "send_count": draw_send_count(jax.random.fold_in(key_list[7], 71), 0),
    }


step_size = 0.3

def reference(table, accum, grad_pooled, sample_slot, row_slot, weight, send_count):
    feat_count = table.shape[0]
    peer_count = send_count.shape[1]
    slot_count = sample_slot.shape[3]
    own_samples = grad_pooled.shape[2] // peer_count
    row_local = table.shape[2] // peer_count
    slot_index = lax.broadcasted_iota(jnp.int32, sample_slot.shape, 3)
    live_mask = slot_index < send_count[..., None]
    live_weights = jnp.where(live_mask, weight, 0).astype(jnp.float32)
    source = lax.broadcasted_iota(jnp.int32, sample_slot.shape, 1)
    owner_index = lax.broadcasted_iota(jnp.int32, sample_slot.shape, 2)
    global_row = (source * row_local + row_slot).astype(jnp.int32)
    target = (owner_index * own_samples + sample_slot).astype(jnp.int32)
    pooled_list = []
    table_list = []
    accum_list = []
    for feature in range(feat_count):
        table_rows = table[feature].astype(jnp.float32)
        grad_rows = grad_pooled[feature].astype(jnp.float32)

        def accumulate(state_pair, entry_group):
            pooled, row_grad = state_pair
            row_index, target_index, weight_row = entry_group
            row_index = row_index.reshape(-1)
            target_index = target_index.reshape(-1)
            weight_row = weight_row.reshape(-1)
            pooled = pooled.at[:, target_index].add(table_rows[:, row_index] * weight_row[None, :])
            row_grad = row_grad.at[:, row_index].add(grad_rows[:, target_index] * weight_row[None, :])
            return ((pooled, row_grad), None)
        start_state = (jnp.zeros((D, peer_count * own_samples), jnp.float32), jnp.zeros((D, peer_count * row_local), jnp.float32))
        (pooled, row_grad), _ = lax.scan(accumulate, start_state, (global_row[feature], target[feature], live_weights[feature]))
        new_accum = accum[feature] + lax.optimization_barrier(jnp.sum(row_grad * row_grad, axis=0)) / D
        new_rows = (table_rows - step_size * row_grad / jnp.sqrt(new_accum)[None, :]).astype(jnp.bfloat16)
        pooled_list.append(pooled)
        table_list.append(new_rows)
        accum_list.append(new_accum)
    return (jnp.stack(pooled_list), jnp.stack(table_list), jnp.stack(accum_list))
```

```python
import jax
import jax.numpy as jnp
from jax import lax
from jax.experimental import pallas as pl
from jax.experimental.pallas import tpu as pltpu
from jax.sharding import PartitionSpec as P

D = 256
STEP = 0.3
H = 8
F32 = jnp.float32
BF = jnp.bfloat16
NT = (((1,), (1,)), ((), ()))
MESH = pl.DeviceIdType.MESH
Z, Y, C, X = 8, 4, 2, 4


def one():
    return jnp.ones((), BF)


def zero():
    return jnp.zeros((), BF)


def lay_out(row_ref, smp_ref, wgt_ref, cnt_ref, rows, slots, weights):
    eye = lax.broadcasted_iota(jnp.int32, (64, 64), 0) == lax.broadcasted_iota(jnp.int32, (64, 64), 1)
    count = jnp.where(eye, jnp.broadcast_to(cnt_ref[...], (64, 64)), 0).astype(F32)
    count = jnp.sum(count, axis=1, keepdims=True).astype(jnp.int32)
    lane = lax.broadcasted_iota(jnp.int32, (64, 128), 1)
    main = jnp.where(lane < count, wgt_ref[:, :128], 0)
    lane = lax.broadcasted_iota(jnp.int32, (64, 32), 1) + 128
    tail = jnp.where(lane < count, wgt_ref[:, 128:160], 0)
    for dst, m, t in (
        (rows, row_ref[:, :128], row_ref[:, 128:160]),
        (slots, smp_ref[:, :128], smp_ref[:, 128:160]),
        (weights, main, tail),
    ):
        dst[0:64, :] = m.astype(F32)
        t = t.astype(F32)
        for k in range(2):
            parts = [t[(4 * k + z) * 8 : (4 * k + z + 1) * 8, :] for z in range(4)]
            dst[64 + 8 * k : 72 + 8 * k, :] = jnp.concatenate(parts, axis=1)


def high_low(r, L):
    h = jnp.floor(r * (1.0 / L))
    return h, r - h * L


def lookup(s, L, rows, slots, weights, t2, oh, xs, put):
    iota = lax.broadcasted_iota(jnp.int32, (256, 128), 0).astype(F32).astype(BF)
    high = []
    for t in range(10):
        h, low = high_low(rows[pl.ds(t * 8 + s, 1), :], L)
        high.append(h)
        for k in range(L // 256):
            key = (low - 256.0 * k).astype(BF)
            oh[k * 256 : (k + 1) * 256, t * 128 : (t + 1) * 128] = jnp.where(iota == key, one(), zero())
    x2 = jnp.dot(t2[...], oh[...], preferred_element_type=F32)
    for t in range(10):
        cols = slice(t * 128, (t + 1) * 128)
        x = x2[0:64, cols]
        for h in range(1, H):
            x = jnp.where(high[t] == float(h), x2[h * 64 : (h + 1) * 64, cols], x)
        x = x.astype(BF)
        if t < 8:
            xs[:, t * 256 : t * 256 + 128] = x
        else:
            for z in range((t - 8) * 4, (t - 8) * 4 + 4):
                xs[:, z * 256 + 128 : z * 256 + 256] = x
    sample = lax.broadcasted_iota(jnp.int32, (128, 128), 0).astype(F32).astype(BF)
    lane = lax.broadcasted_iota(jnp.int32, (1, 128), 1)
    for z in range(8):
        at, tail = z * 8 + s, (8 + z // 4) * 8 + s
        mine = (lane >= 32 * (z % 4)) & (lane < 32 * (z % 4) + 32)
        tail_w = jnp.where(mine, weights[pl.ds(tail, 1), :], 0.0).astype(BF)
        spread = jnp.concatenate(
            [
                jnp.where(sample == slots[pl.ds(at, 1), :].astype(BF), weights[pl.ds(at, 1), :].astype(BF), zero()),
                jnp.where(sample == slots[pl.ds(tail, 1), :].astype(BF), tail_w, zero()),
            ],
            axis=1,
        )
        put(z, lax.dot_general(xs[:, z * 256 : (z + 1) * 256], spread, NT, preferred_element_type=F32))


def gradient(s, L, grad, rows, slots, weights, a, wr, acc):
    iota = lax.broadcasted_iota(jnp.int32, (256, 128), 0).astype(F32).astype(BF)
    lane = lax.broadcasted_iota(jnp.int32, (1, 128), 1)
    for t in range(10):
        cols = slice(t * 128, (t + 1) * 128)
        h, low = high_low(rows[pl.ds(t * 8 + s, 1), :], L)
        h = h.astype(BF)
        w = weights[pl.ds(t * 8 + s, 1), :].astype(BF)
        for k in range(L // 256):
            key = (low - 256.0 * k).astype(BF)
            wr[k * 256 : (k + 1) * 256, cols] = jnp.where(iota == key, w, zero())
        index = jnp.broadcast_to(slots[pl.ds(t * 8 + s, 1), :].astype(jnp.int32), (64, 128))

        def pick(z):
            return jnp.take_along_axis(grad(z).astype(F32), index, axis=1, mode="promise_in_bounds")

        if t < 8:
            e = pick(t)
        else:
            e = pick((t - 8) * 4)
            for z in range(1, 4):
                e = jnp.where(lane >= 32 * z, pick((t - 8) * 4 + z), e)
        e = e.astype(BF)
        for k in range(H):
            a[k * 64 : (k + 1) * 64, cols] = jnp.where(h == jnp.asarray(float(k), BF), e, zero())
    acc[...] += lax.dot_general(a[...], wr[...], NT, preferred_element_type=F32)


def kernel(
    tab, accum, g, smp, row, wgt, cnt,
    pooled, new_tab, new_accum,
    rows, slots, weights, t2, oh, xs, a, acc,
    gall, part, from_core, from_y, from_z, squares,
    gz_s, gz_r, gy_s, gy_r, gc_s, gc_r, pc_s, pc_r, py_s, py_r, pz_s, pz_r, sx_s, sx_r,
):
    L = tab.shape[1] // H
    r, x = lax.axis_index("rows"), lax.axis_index("dims")
    z, y, c = r // (Y * C), lax.rem(r // C, Y), lax.rem(r, C)

    def z_at(d):
        return (lax.rem(z + d, Z) * (Y * C) + y * C + c, x)

    def y_at(d):
        return (z * (Y * C) + lax.rem(y + d, Y) * C + c, x)

    def x_at(d):
        return (r, lax.rem(x + d, X))

    sibling = (z * (Y * C) + y * C + (1 - c), x)

    def copy(src, dst, send, recv, to):
        return pltpu.make_async_remote_copy(
            src_ref=src, dst_ref=dst, send_sem=send, recv_sem=recv, device_id=to, device_id_type=MESH
        )

    barrier = pltpu.get_barrier_semaphore()
    peers = [z_at(d) for d in range(1, Z)] + [y_at(d) for d in range(1, Y)] + [sibling]
    peers += [x_at(d) for d in range(1, X)]
    for to in peers:
        pl.semaphore_signal(barrier, inc=1, device_id=to, device_id_type=MESH)

    gall[c, y, z] = g[...]
    lay_out(row, smp, wgt, cnt, rows, slots, weights)
    for h in range(H):
        t2[h * 64 : (h + 1) * 64, :] = tab[:, h * L : (h + 1) * L]
    acc[...] = jnp.zeros_like(acc)

    pl.semaphore_wait(barrier, len(peers))

    along_z = [
        copy(g, gall.at[c, y, z], gz_s.at[d - 1], gz_r.at[d - 1], z_at(d)) for d in range(1, Z)
    ]
    along_y = [
        copy(gall.at[c, y], gall.at[c, y], gy_s.at[d - 1], gy_r.at[d - 1], y_at(d)) for d in range(1, Y)
    ]
    to_core = copy(gall.at[c], gall.at[c], gc_s.at[0], gc_r.at[0], sibling)
    for each in along_z:
        each.start()

    def look(q, side):
        block = lax.rem(y + 1 + q, Y)

        def put(k, value):
            part[side, block, k] = value

        lookup(block * C + side, L, rows, slots, weights, t2, oh, xs, put)
        return block

    def to_sibling(q):
        block = lax.rem(y + 1 + q, Y)
        return copy(part.at[1 - c, block], from_core.at[q], pc_s.at[q], pc_r.at[q], sibling)

    def to_y(q):
        return copy(
            part.at[c, lax.rem(y + 1 + q, Y)], from_y.at[q], py_s.at[q], py_r.at[q], y_at(q + 1)
        )

    def to_z(d):
        return copy(
            part.at[c, y, lax.rem(z + d, Z)], from_z.at[d - 1], pz_s.at[d - 1], pz_r.at[d - 1], z_at(d)
        )

    @pl.loop(0, 2 * Y)
    def _(i):
        q = lax.rem(i, Y)
        side = jnp.where(i < Y, 1 - c, c)
        block = look(q, side)

        @pl.when(i < Y)
        def _():
            to_sibling(q).start()

        @pl.when(i >= Y)
        def _():
            to_sibling(q).wait_recv()
            part[c, block] += from_core[q]

        @pl.when((i >= Y) & (i < 2 * Y - 1))
        def _():
            to_y(q).start()

        @pl.when(i == 2)
        def _():
            for each in along_z:
                each.wait_recv()
            for each in along_y:
                each.start()

        @pl.when(i == 5)
        def _():
            for each in along_y:
                each.wait_recv()
            to_core.start()

    @pl.loop(0, 2 * Y)
    def _(i):
        side = jnp.where(i < Y, c, 1 - c)
        block = lax.rem(i, Y)

        @pl.when(i == Y)
        def _():
            to_core.wait_recv()

        @pl.when(i == 3)
        def _():
            for q in range(Y - 1):
                to_y(q).wait_recv()
            part[c, y] += from_y[0] + from_y[1] + from_y[2]
            for d in range(1, Z):
                to_z(d).start()

        gradient(block * C + side, L, lambda k: gall[side, block, k], rows, slots, weights, a, oh, acc)

    for h in range(H):
        v = acc[h * 64 : (h + 1) * 64, :]
        squares[x, h : h + 1, :] = jnp.sum(v * v, axis=0, keepdims=True)
    along_x = [
        copy(squares.at[x], squares.at[x], sx_s.at[d - 1], sx_r.at[d - 1], x_at(d)) for d in range(1, X)
    ]
    for each in along_x:
        each.start()

    for d in range(1, Z):
        to_z(d).wait_recv()
    total = part[c, y, z]
    for d in range(1, Z):
        total += from_z[d - 1]
    pooled[...] = total

    for each in along_x:
        each.wait_recv()
    norm = (squares[0] + squares[1]) + (squares[2] + squares[3])
    for h in range(H):
        cols = slice(h * L, (h + 1) * L)
        new = accum[:, cols] + norm[h : h + 1, :] / D
        new_accum[:, cols] = new
        moved = acc[h * 64 : (h + 1) * 64, :] * (STEP * lax.rsqrt(new))
        new_tab[:, cols] = (tab[:, cols].astype(F32) - moved).astype(BF)

    for each in along_z + along_y + [to_core] + along_x:
        each.wait_send()
    for q in range(Y):
        to_sibling(q).wait_send()
    for q in range(Y - 1):
        to_y(q).wait_send()
    for d in range(1, Z):
        to_z(d).wait_send()


def shards(table, accum, grad_pooled, sample_slot, row_slot, weight, send_count):
    _, dim, n_rows = table.shape
    own = grad_pooled.shape[2]
    L = n_rows // H
    vmem = pl.BlockSpec(memory_space=pltpu.VMEM)
    dma = pltpu.SemaphoreType.DMA
    pooled, new_table, new_accum = pl.pallas_call(
        kernel,
        out_shape=(
            jax.ShapeDtypeStruct((dim, own), F32),
            jax.ShapeDtypeStruct((dim, n_rows), BF),
            jax.ShapeDtypeStruct((1, n_rows), F32),
        ),
        in_specs=[vmem] * 7,
        out_specs=(vmem,) * 3,
        scratch_shapes=[pltpu.VMEM((80, 128), F32)] * 3
        + [
            pltpu.VMEM((64 * H, L), BF),
            pltpu.VMEM((L, 1280), BF),
            pltpu.VMEM((64, 2048), BF),
            pltpu.VMEM((64 * H, 1280), BF),
            pltpu.VMEM((64 * H, L), F32),
            pltpu.VMEM((C, Y, Z, dim, own), BF),
            pltpu.VMEM((C, Y, Z, dim, own), F32),
            pltpu.VMEM((Y, Z, dim, own), F32),
            pltpu.VMEM((Y - 1, Z, dim, own), F32),
            pltpu.VMEM((Z - 1, dim, own), F32),
            pltpu.VMEM((X, H, L), F32),
        ]
        + [dma((n,)) for n in (7, 7, 3, 3, 1, 1, 4, 4, 3, 3, 7, 7, 3, 3)],
        compiler_params=pltpu.CompilerParams(
            collective_id=0, has_side_effects=True, vmem_limit_bytes=40 << 20
        ),
    )(
        table[0],
        accum,
        grad_pooled[0],
        sample_slot[0, 0],
        row_slot[0, 0],
        weight[0, 0],
        send_count[0],
    )
    return pooled[None], new_table[None], new_accum


def solution(mesh):
    return jax.shard_map(
        shards,
        mesh=mesh,
        in_specs=(
            P(None, "dims", "rows"),
            P(None, "rows"),
            P(None, "dims", "rows"),
            P(None, "rows", None, None),
            P(None, "rows", None, None),
            P(None, "rows", None, None),
            P(None, "rows", None),
        ),
        out_specs=(P(None, "dims", "rows"), P(None, "dims", "rows"), P(None, "rows")),
        check_vma=False,
    )
```

```python
import jax
import jax.numpy as jnp
from jax import lax
from jax.experimental import pallas as pl
from jax.experimental.pallas import tpu as pltpu
from jax.sharding import PartitionSpec as P

D = 256
STEP = 0.3
H = 8
F32 = jnp.float32
BF = jnp.bfloat16
NT = (((1,), (1,)), ((), ()))
MESH = pl.DeviceIdType.MESH
Z, Y, C, X = 8, 4, 2, 4


def one():
    return jnp.ones((), BF)


def zero():
    return jnp.zeros((), BF)


def lay_out(row_ref, smp_ref, wgt_ref, cnt_ref, rows, slots, weights):
    eye = lax.broadcasted_iota(jnp.int32, (64, 64), 0) == lax.broadcasted_iota(jnp.int32, (64, 64), 1)
    count = jnp.where(eye, jnp.broadcast_to(cnt_ref[...], (64, 64)), 0).astype(F32)
    count = jnp.sum(count, axis=1, keepdims=True).astype(jnp.int32)
    lane = lax.broadcasted_iota(jnp.int32, (64, 128), 1)
    main = jnp.where(lane < count, wgt_ref[:, :128], 0)
    lane = lax.broadcasted_iota(jnp.int32, (64, 32), 1) + 128
    tail = jnp.where(lane < count, wgt_ref[:, 128:160], 0)
    for dst, m, t in (
        (rows, row_ref[:, :128], row_ref[:, 128:160]),
        (slots, smp_ref[:, :128], smp_ref[:, 128:160]),
        (weights, main, tail),
    ):
        dst[0:64, :] = m.astype(F32)
        t = t.astype(F32)
        for k in range(2):
            parts = [t[(4 * k + z) * 8 : (4 * k + z + 1) * 8, :] for z in range(4)]
            dst[64 + 8 * k : 72 + 8 * k, :] = jnp.concatenate(parts, axis=1)


def high_low(r, L):
    h = jnp.floor(r * (1.0 / L))
    return h, r - h * L


def lookup(s, L, rows, slots, weights, t2, oh, xs, put):
    iota = lax.broadcasted_iota(jnp.int32, (256, 128), 0).astype(F32).astype(BF)
    high = []
    for t in range(10):
        h, low = high_low(rows[pl.ds(t * 8 + s, 1), :], L)
        high.append(h)
        for k in range(L // 256):
            key = (low - 256.0 * k).astype(BF)
            oh[k * 256 : (k + 1) * 256, t * 128 : (t + 1) * 128] = jnp.where(iota == key, one(), zero())
    x2 = jnp.dot(t2[...], oh[...], preferred_element_type=F32)
    for t in range(10):
        cols = slice(t * 128, (t + 1) * 128)
        x = x2[0:64, cols]
        for h in range(1, H):
            x = jnp.where(high[t] == float(h), x2[h * 64 : (h + 1) * 64, cols], x)
        x = x.astype(BF)
        if t < 8:
            xs[:, t * 256 : t * 256 + 128] = x
        else:
            for z in range((t - 8) * 4, (t - 8) * 4 + 4):
                xs[:, z * 256 + 128 : z * 256 + 256] = x
    sample = lax.broadcasted_iota(jnp.int32, (128, 128), 0).astype(F32).astype(BF)
    lane = lax.broadcasted_iota(jnp.int32, (1, 128), 1)
    for z in range(8):
        at, tail = z * 8 + s, (8 + z // 4) * 8 + s
        mine = (lane >= 32 * (z % 4)) & (lane < 32 * (z % 4) + 32)
        tail_w = jnp.where(mine, weights[pl.ds(tail, 1), :], 0.0).astype(BF)
        spread = jnp.concatenate(
            [
                jnp.where(sample == slots[pl.ds(at, 1), :].astype(BF), weights[pl.ds(at, 1), :].astype(BF), zero()),
                jnp.where(sample == slots[pl.ds(tail, 1), :].astype(BF), tail_w, zero()),
            ],
            axis=1,
        )
        put(z, lax.dot_general(xs[:, z * 256 : (z + 1) * 256], spread, NT, preferred_element_type=F32))


def gradient(s, L, grad, rows, slots, weights, a, wr, acc):
    iota = lax.broadcasted_iota(jnp.int32, (256, 128), 0).astype(F32).astype(BF)
    lane = lax.broadcasted_iota(jnp.int32, (1, 128), 1)
    for t in range(10):
        cols = slice(t * 128, (t + 1) * 128)
        h, low = high_low(rows[pl.ds(t * 8 + s, 1), :], L)
        h = h.astype(BF)
        w = weights[pl.ds(t * 8 + s, 1), :].astype(BF)
        for k in range(L // 256):
            key = (low - 256.0 * k).astype(BF)
            wr[k * 256 : (k + 1) * 256, cols] = jnp.where(iota == key, w, zero())
        index = jnp.broadcast_to(slots[pl.ds(t * 8 + s, 1), :].astype(jnp.int32), (64, 128))

        def pick(z):
            return jnp.take_along_axis(grad(z).astype(F32), index, axis=1, mode="promise_in_bounds")

        if t < 8:
            e = pick(t)
        else:
            e = pick((t - 8) * 4)
            for z in range(1, 4):
                e = jnp.where(lane >= 32 * z, pick((t - 8) * 4 + z), e)
        e = e.astype(BF)
        for k in range(H):
            a[k * 64 : (k + 1) * 64, cols] = jnp.where(h == jnp.asarray(float(k), BF), e, zero())
    acc[...] += lax.dot_general(a[...], wr[...], NT, preferred_element_type=F32)


def kernel(
    tab_in, accum_in, g, smp_in, row_in, wgt_in, cnt_in,
    pooled_out, new_tab_out, new_accum_out,
    pooled, new_tab, new_accum, store, rows, slots, weights, t2, oh, xs, a, acc,
    gall, part, from_core, from_y, from_z, squares,
    tab, accum, smp, row, wgt, cnt, load, gz_s, gz_r, gy_s, gy_r, gc_s, gc_r, pc_s, pc_r, py_s, py_r, pz_s, pz_r, sx_s, sx_r,
):
    L = tab.shape[1] // H
    pairs = ((cnt_in, cnt), (wgt_in, wgt), (row_in, row), (smp_in, smp), (tab_in, tab), (accum_in, accum))
    loads = [pltpu.make_async_copy(src, dst, load.at[i]) for i, (src, dst) in enumerate(pairs)]
    for each in loads:
        each.start()
    r, x = lax.axis_index("rows"), lax.axis_index("dims")
    z, y, c = r // (Y * C), lax.rem(r // C, Y), lax.rem(r, C)

    def z_at(d):
        return (lax.rem(z + d, Z) * (Y * C) + y * C + c, x)

    def y_at(d):
        return (z * (Y * C) + lax.rem(y + d, Y) * C + c, x)

    def x_at(d):
        return (r, lax.rem(x + d, X))

    sibling = (z * (Y * C) + y * C + (1 - c), x)

    def copy(src, dst, send, recv, to):
        return pltpu.make_async_remote_copy(
            src_ref=src, dst_ref=dst, send_sem=send, recv_sem=recv, device_id=to, device_id_type=MESH
        )

    barrier = pltpu.get_barrier_semaphore()
    peers = [z_at(d) for d in range(1, Z)] + [y_at(d) for d in range(1, Y)] + [sibling]
    peers += [x_at(d) for d in range(1, X)]
    for to in peers:
        pl.semaphore_signal(barrier, inc=1, device_id=to, device_id_type=MESH)

    own_grad = pltpu.make_async_copy(g, gall.at[c, y, z], load.at[len(pairs)])
    own_grad.start()
    acc[...] = jnp.zeros_like(acc)
    for each in loads:
        each.wait()
    own_grad.wait()
    lay_out(row, smp, wgt, cnt, rows, slots, weights)
    for h in range(H):
        t2[h * 64 : (h + 1) * 64, :] = tab[:, h * L : (h + 1) * L]

    pl.semaphore_wait(barrier, len(peers))

    along_z = [
        copy(gall.at[c, y, z], gall.at[c, y, z], gz_s.at[d - 1], gz_r.at[d - 1], z_at(d)) for d in range(1, Z)
    ]

    def block_at(d):
        return lax.rem(y + d, Y)

    half = (pl.ds(0, Z // 2), pl.ds(Z // 2, Z // 2))
    along_y = [
        copy(gall.at[c, y], gall.at[c, y], gy_s.at[0], gy_r.at[0], y_at(1)),
        copy(gall.at[c, y], gall.at[c, y], gy_s.at[1], gy_r.at[1], y_at(3)),
    ]
    further = [
        copy(gall.at[c, block_at(3), half[0]], gall.at[c, block_at(3), half[0]], gy_s.at[2], gy_r.at[2], y_at(1)),
        copy(gall.at[c, block_at(1), half[1]], gall.at[c, block_at(1), half[1]], gy_s.at[3], gy_r.at[3], y_at(3)),
    ]

    def to_core(k):
        block = block_at((0, 1, 3, 2)[k])
        return copy(gall.at[c, block], gall.at[c, block], gc_s.at[k], gc_r.at[k], sibling)

    for each in along_z:
        each.start()

    def to_sibling(q):
        block = block_at(jnp.where(q < 2, q + 2, 3 - q))
        return copy(part.at[1 - c, block], from_core.at[q], pc_s.at[q], pc_r.at[q], sibling)

    two_on = [
        copy(part.at[c, block_at(2), half[0]], from_y.at[0, half[0]], py_s.at[0], py_r.at[0], y_at(1)),
        copy(part.at[c, block_at(2), half[1]], from_y.at[0, half[1]], py_s.at[1], py_r.at[1], y_at(3)),
    ]
    one_on = [
        copy(part.at[c, block_at(1)], from_y.at[1], py_s.at[2], py_r.at[2], y_at(1)),
        copy(part.at[c, block_at(3)], from_y.at[2], py_s.at[3], py_r.at[3], y_at(3)),
    ]

    def to_z(d):
        return copy(
            part.at[c, y, lax.rem(z + d, Z)], from_z.at[d - 1], pz_s.at[d - 1], pz_r.at[d - 1], z_at(d)
        )

    @pl.loop(0, 2 * Y)
    def _(i):
        q = lax.rem(i, Y)
        side = jnp.where(i < Y, 1 - c, c)
        block = block_at(jnp.where(q < 2, q + 2, 3 - q))

        def put(k, value):
            part[side, block, k] = value

        lookup(block * C + side, L, rows, slots, weights, t2, oh, xs, put)

        @pl.when(i < Y)
        def _():
            to_sibling(q).start()

        @pl.when(i >= Y)
        def _():
            to_sibling(q).wait_recv()
            part[c, block] += from_core[q]

        @pl.when(i == 3)
        def _():
            for each in along_z:
                each.wait_recv()
            for each in along_y:
                each.start()
            to_core(0).start()

        @pl.when(i == Y)
        def _():
            for each in two_on:
                each.start()

        @pl.when(i == 6)
        def _():
            for each in along_y:
                each.wait_recv()
            for each in further:
                each.start()
            to_core(1).start()
            to_core(2).start()
            two_on[1].wait_recv()
            part[c, block_at(3), half[1]] += from_y[0, half[1]]
            one_on[1].start()

        @pl.when(i == 7)
        def _():
            two_on[0].wait_recv()
            part[c, block_at(1), half[0]] += from_y[0, half[0]]
            one_on[0].start()

    @pl.loop(0, 2 * Y)
    def _(i):
        k = lax.rem(i, Y)
        side = jnp.where(i < Y, c, 1 - c)
        block = block_at(jnp.where(k < 2, k, 5 - k))

        @pl.when(i == 3)
        def _():
            for each in further:
                each.wait_recv()
            to_core(3).start()

        for n in range(Y):

            @pl.when(i == Y + n)
            def _():
                to_core(n).wait_recv()

        gradient(block * C + side, L, lambda n: gall[side, block, n], rows, slots, weights, a, oh, acc)

        @pl.when(i == 5)
        def _():
            for each in one_on:
                each.wait_recv()
            part[c, y] += from_y[1] + from_y[2]
            for d in range(1, Z):
                to_z(d).start()

    for h in range(H):
        v = acc[h * 64 : (h + 1) * 64, :]
        squares[x, h : h + 1, :] = jnp.sum(v * v, axis=0, keepdims=True)
    along_x = [
        copy(squares.at[x], squares.at[x], sx_s.at[d - 1], sx_r.at[d - 1], x_at(d)) for d in range(1, X)
    ]
    for each in along_x:
        each.start()

    for d in range(1, Z):
        to_z(d).wait_recv()
    total = part[c, y, z]
    for d in range(1, Z):
        total += from_z[d - 1]
    pooled[...] = total
    out = [pltpu.make_async_copy(pooled, pooled_out, store.at[0])]
    out[0].start()

    for each in along_x:
        each.wait_recv()
    norm = (squares[0] + squares[1]) + (squares[2] + squares[3])
    for h in range(H):
        cols = slice(h * L, (h + 1) * L)
        new = accum[:, cols] + norm[h : h + 1, :] / D
        new_accum[:, cols] = new
        moved = acc[h * 64 : (h + 1) * 64, :] * (STEP * lax.rsqrt(new))
        new_tab[:, cols] = (tab[:, cols].astype(F32) - moved).astype(BF)
    out += [
        pltpu.make_async_copy(new_tab, new_tab_out, store.at[1]),
        pltpu.make_async_copy(new_accum, new_accum_out, store.at[2]),
    ]
    out[1].start()
    out[2].start()

    for each in along_z + along_y + further + two_on + one_on + along_x:
        each.wait_send()
    for q in range(Y):
        to_core(q).wait_send()
        to_sibling(q).wait_send()
    for d in range(1, Z):
        to_z(d).wait_send()
    for each in out:
        each.wait()


def hand_on(*refs):
    n = (len(refs) - 2) // 3
    src, dst, held, come, go = refs[:n], refs[n : 2 * n], refs[2 * n : 3 * n], refs[-2], refs[-1]
    loads = [pltpu.make_async_copy(src[i], held[i], come.at[i]) for i in range(n)]
    stores = [pltpu.make_async_copy(held[i], dst[i], go.at[i]) for i in range(n)]
    for each in loads:
        each.start()
    for i in range(n):
        loads[i].wait()
        stores[i].start()
    for each in stores:
        each.wait()


def shards(table, accum, grad_pooled, sample_slot, row_slot, weight, send_count):
    _, dim, n_rows = table.shape
    own = grad_pooled.shape[2]
    L = n_rows // H
    dma = pltpu.SemaphoreType.DMA
    anywhere = pl.BlockSpec(memory_space=pl.ANY)
    shapes = (
        jax.ShapeDtypeStruct((dim, own), F32),
        jax.ShapeDtypeStruct((dim, n_rows), BF),
        jax.ShapeDtypeStruct((1, n_rows), F32),
    )
    results = pl.pallas_call(
        kernel,
        out_shape=shapes,
        in_specs=[anywhere] * 7,
        out_specs=(anywhere,) * 3,
        scratch_shapes=[pltpu.VMEM(each.shape, each.dtype) for each in shapes]
        + [dma((3,))]
        + [pltpu.VMEM((80, 128), F32)] * 3
        + [
            pltpu.VMEM((64 * H, L), BF),
            pltpu.VMEM((L, 1280), BF),
            pltpu.VMEM((64, 2048), BF),
            pltpu.VMEM((64 * H, 1280), BF),
            pltpu.VMEM((64 * H, L), F32),
            pltpu.VMEM((C, Y, Z, dim, own), BF),
            pltpu.VMEM((C, Y, Z, dim, own), F32),
            pltpu.VMEM((Y, Z, dim, own), F32),
            pltpu.VMEM((3, Z, dim, own), F32),
            pltpu.VMEM((Z - 1, dim, own), F32),
            pltpu.VMEM((X, H, L), F32),
        ]
        + [pltpu.VMEM((dim, n_rows), BF), pltpu.VMEM((1, n_rows), F32)]
        + [pltpu.VMEM(sample_slot.shape[2:], jnp.int32)] * 3
        + [pltpu.VMEM(send_count.shape[1:], jnp.int32)]
        + [dma((n,)) for n in (7, 7, 7, 4, 4, 4, 4, 4, 4, 4, 4, 7, 7, 3, 3)],
        compiler_params=pltpu.CompilerParams(
            collective_id=0, has_side_effects=True, vmem_limit_bytes=64 << 20
        ),
    )(
        table[0],
        accum,
        grad_pooled[0],
        sample_slot[0, 0],
        row_slot[0, 0],
        weight[0, 0],
        send_count[0],
    )
    pooled, new_table, new_accum = pl.pallas_call(
        hand_on,
        out_shape=shapes,
        in_specs=[anywhere] * 3,
        out_specs=(anywhere,) * 3,
        scratch_shapes=[pltpu.VMEM(each.shape, each.dtype) for each in shapes] + [dma((3,)), dma((3,))],
        compiler_params=pltpu.CompilerParams(vmem_limit_bytes=64 << 20),
    )(*results)
    return pooled[None], new_table[None], new_accum


def solution(mesh):
    return jax.shard_map(
        shards,
        mesh=mesh,
        in_specs=(
            P(None, "dims", "rows"),
            P(None, "rows"),
            P(None, "dims", "rows"),
            P(None, "rows", None, None),
            P(None, "rows", None, None),
            P(None, "rows", None, None),
            P(None, "rows", None),
        ),
        out_specs=(P(None, "dims", "rows"), P(None, "dims", "rows"), P(None, "rows")),
        check_vma=False,
    )
```

```python
import jax
import jax.numpy as jnp
from jax import lax
from jax.experimental import pallas as pl
from jax.experimental.pallas import tpu as pltpu
from jax.sharding import PartitionSpec as P

D = 256
STEP = 0.3
H = 8
F32 = jnp.float32
BF = jnp.bfloat16
NT = (((1,), (1,)), ((), ()))
MESH = pl.DeviceIdType.MESH
Z, Y, C, X = 8, 4, 2, 4


def one():
    return jnp.ones((), BF)


def zero():
    return jnp.zeros((), BF)


def lay_out(row_ref, smp_ref, wgt_ref, cnt_ref, rows, slots, weights):
    eye = lax.broadcasted_iota(jnp.int32, (64, 64), 0) == lax.broadcasted_iota(jnp.int32, (64, 64), 1)
    count = jnp.where(eye, jnp.broadcast_to(cnt_ref[...], (64, 64)), 0).astype(F32)
    count = jnp.sum(count, axis=1, keepdims=True).astype(jnp.int32)
    lane = lax.broadcasted_iota(jnp.int32, (64, 128), 1)
    main = jnp.where(lane < count, wgt_ref[:, :128], 0)
    lane = lax.broadcasted_iota(jnp.int32, (64, 32), 1) + 128
    tail = jnp.where(lane < count, wgt_ref[:, 128:160], 0)
    for dst, m, t in (
        (rows, row_ref[:, :128], row_ref[:, 128:160]),
        (slots, smp_ref[:, :128], smp_ref[:, 128:160]),
        (weights, main, tail),
    ):
        dst[0:64, :] = m.astype(F32)
        t = t.astype(F32)
        for k in range(2):
            parts = [t[(4 * k + z) * 8 : (4 * k + z + 1) * 8, :] for z in range(4)]
            dst[64 + 8 * k : 72 + 8 * k, :] = jnp.concatenate(parts, axis=1)


def high_low(r, L):
    h = jnp.floor(r * (1.0 / L))
    return h, r - h * L


def lookup(s, L, rows, slots, weights, t2, oh, xs, put):
    iota = lax.broadcasted_iota(jnp.int32, (256, 128), 0).astype(F32).astype(BF)
    high = []
    for t in range(10):
        h, low = high_low(rows[pl.ds(t * 8 + s, 1), :], L)
        high.append(h)
        for k in range(L // 256):
            key = (low - 256.0 * k).astype(BF)
            oh[k * 256 : (k + 1) * 256, t * 128 : (t + 1) * 128] = jnp.where(iota == key, one(), zero())
    x2 = jnp.dot(t2[...], oh[...], preferred_element_type=F32)
    for t in range(10):
        cols = slice(t * 128, (t + 1) * 128)
        x = x2[0:64, cols]
        for h in range(1, H):
            x = jnp.where(high[t] == float(h), x2[h * 64 : (h + 1) * 64, cols], x)
        x = x.astype(BF)
        if t < 8:
            xs[:, t * 256 : t * 256 + 128] = x
        else:
            for z in range((t - 8) * 4, (t - 8) * 4 + 4):
                xs[:, z * 256 + 128 : z * 256 + 256] = x
    sample = lax.broadcasted_iota(jnp.int32, (128, 128), 0).astype(F32).astype(BF)
    lane = lax.broadcasted_iota(jnp.int32, (1, 128), 1)
    for z in range(8):
        at, tail = z * 8 + s, (8 + z // 4) * 8 + s
        mine = (lane >= 32 * (z % 4)) & (lane < 32 * (z % 4) + 32)
        tail_w = jnp.where(mine, weights[pl.ds(tail, 1), :], 0.0).astype(BF)
        spread = jnp.concatenate(
            [
                jnp.where(sample == slots[pl.ds(at, 1), :].astype(BF), weights[pl.ds(at, 1), :].astype(BF), zero()),
                jnp.where(sample == slots[pl.ds(tail, 1), :].astype(BF), tail_w, zero()),
            ],
            axis=1,
        )
        put(z, lax.dot_general(xs[:, z * 256 : (z + 1) * 256], spread, NT, preferred_element_type=F32))


def gradient(s, L, grad, rows, slots, weights, a, wr, acc):
    iota = lax.broadcasted_iota(jnp.int32, (256, 128), 0).astype(F32).astype(BF)
    lane = lax.broadcasted_iota(jnp.int32, (1, 128), 1)
    for t in range(10):
        cols = slice(t * 128, (t + 1) * 128)
        h, low = high_low(rows[pl.ds(t * 8 + s, 1), :], L)
        h = h.astype(BF)
        w = weights[pl.ds(t * 8 + s, 1), :].astype(BF)
        for k in range(L // 256):
            key = (low - 256.0 * k).astype(BF)
            wr[k * 256 : (k + 1) * 256, cols] = jnp.where(iota == key, w, zero())
        index = jnp.broadcast_to(slots[pl.ds(t * 8 + s, 1), :].astype(jnp.int32), (64, 128))

        def pick(z):
            return jnp.take_along_axis(grad(z).astype(F32), index, axis=1, mode="promise_in_bounds")

        if t < 8:
            e = pick(t)
        else:
            e = pick((t - 8) * 4)
            for z in range(1, 4):
                e = jnp.where(lane >= 32 * z, pick((t - 8) * 4 + z), e)
        e = e.astype(BF)
        for k in range(H):
            a[k * 64 : (k + 1) * 64, cols] = jnp.where(h == jnp.asarray(float(k), BF), e, zero())
    acc[...] += lax.dot_general(a[...], wr[...], NT, preferred_element_type=F32)


def pack(values, dst):
    n, dim, own = values.shape
    row = lax.broadcasted_iota(jnp.int32, (16, own), 0)
    exponents = jnp.zeros((16, own), F32)
    for j in range(n):
        top = jnp.max(jnp.abs(values[j]), axis=0, keepdims=True)
        e = jnp.ceil(jnp.log2(jnp.maximum(top, 1e-30)))
        dst[j * dim : (j + 1) * dim, :] = jnp.round(values[j] * jnp.exp2(14.0 - e)).astype(jnp.int32).astype(jnp.int16)
        exponents = jnp.where(row == j, e, exponents)
    dst[n * dim : n * dim + 16, :] = exponents.astype(jnp.int32).astype(jnp.int16)


def unpack(src, n):
    dim = (src.shape[0] - 16) // n
    exponents = src[n * dim : n * dim + 16, :].astype(jnp.int32).astype(F32)
    return [
        src[j * dim : (j + 1) * dim, :].astype(jnp.int32).astype(F32) * jnp.exp2(exponents[j : j + 1, :] - 14.0)
        for j in range(n)
    ]


def kernel(
    tab_in, accum_in, g, smp_in, row_in, wgt_in, cnt_in,
    pooled_out, new_tab_out, new_accum_out,
    pooled, new_tab, new_accum, store, rows, slots, weights, t2, oh, xs, a, acc,
    gall, part, from_core, two_out, two_in, one_out, one_in, z_out, z_in, squares,
    tab, accum, smp, row, wgt, cnt, load, gz_s, gz_r, gy_s, gy_r, gc_s, gc_r, pc_s, pc_r, py_s, py_r, pz_s, pz_r, sx_s, sx_r,
):
    L = tab.shape[1] // H
    pairs = ((cnt_in, cnt), (wgt_in, wgt), (row_in, row), (smp_in, smp), (tab_in, tab), (accum_in, accum))
    loads = [pltpu.make_async_copy(src, dst, load.at[i]) for i, (src, dst) in enumerate(pairs)]
    for each in loads:
        each.start()
    r, x = lax.axis_index("rows"), lax.axis_index("dims")
    z, y, c = r // (Y * C), lax.rem(r // C, Y), lax.rem(r, C)

    def z_at(d):
        return (lax.rem(z + d, Z) * (Y * C) + y * C + c, x)

    def y_at(d):
        return (z * (Y * C) + lax.rem(y + d, Y) * C + c, x)

    def x_at(d):
        return (r, lax.rem(x + d, X))

    sibling = (z * (Y * C) + y * C + (1 - c), x)

    def copy(src, dst, send, recv, to):
        return pltpu.make_async_remote_copy(
            src_ref=src, dst_ref=dst, send_sem=send, recv_sem=recv, device_id=to, device_id_type=MESH
        )

    barrier = pltpu.get_barrier_semaphore()
    peers = [z_at(d) for d in range(1, Z)] + [y_at(d) for d in range(1, Y)] + [sibling]
    peers += [x_at(d) for d in range(1, X)]
    for to in peers:
        pl.semaphore_signal(barrier, inc=1, device_id=to, device_id_type=MESH)

    own_grad = pltpu.make_async_copy(g, gall.at[c, y, z], load.at[len(pairs)])
    own_grad.start()
    acc[...] = jnp.zeros_like(acc)
    own_grad.wait()
    pl.semaphore_wait(barrier, len(peers))

    along_z = [
        copy(gall.at[c, y, z], gall.at[c, y, z], gz_s.at[d - 1], gz_r.at[d - 1], z_at(d)) for d in range(1, Z)
    ]

    def block_at(d):
        return lax.rem(y + d, Y)

    half = (pl.ds(0, Z // 2), pl.ds(Z // 2, Z // 2))
    along_y = [
        copy(gall.at[c, y], gall.at[c, y], gy_s.at[0], gy_r.at[0], y_at(1)),
        copy(gall.at[c, y], gall.at[c, y], gy_s.at[1], gy_r.at[1], y_at(3)),
    ]
    further = [
        copy(gall.at[c, block_at(3), half[0]], gall.at[c, block_at(3), half[0]], gy_s.at[2], gy_r.at[2], y_at(1)),
        copy(gall.at[c, block_at(1), half[1]], gall.at[c, block_at(1), half[1]], gy_s.at[3], gy_r.at[3], y_at(3)),
    ]

    def to_core(k):
        block = block_at((0, 1, 3, 2)[k])
        return copy(gall.at[c, block], gall.at[c, block], gc_s.at[k], gc_r.at[k], sibling)

    for each in along_z:
        each.start()

    for each in loads:
        each.wait()
    lay_out(row, smp, wgt, cnt, rows, slots, weights)
    for h in range(H):
        t2[h * 64 : (h + 1) * 64, :] = tab[:, h * L : (h + 1) * L]

    def to_sibling(q):
        block = block_at(jnp.where(q < 2, q + 2, 3 - q))
        return copy(part.at[1 - c, block], from_core.at[q], pc_s.at[q], pc_r.at[q], sibling)

    two_on = [copy(two_out.at[n], two_in.at[n], py_s.at[n], py_r.at[n], y_at((1, 3)[n])) for n in range(2)]
    one_on = [copy(one_out.at[n], one_in.at[n], py_s.at[2 + n], py_r.at[2 + n], y_at((1, 3)[n])) for n in range(2)]

    def add(block, n, packed):
        values = unpack(packed, Z // 2)
        for j in range(Z // 2):
            part[c, block, n * (Z // 2) + j] += values[j]

    def to_z(d):
        return copy(z_out.at[d - 1], z_in.at[d - 1], pz_s.at[d - 1], pz_r.at[d - 1], z_at(d))

    @pl.loop(0, 2 * Y)
    def _(i):
        q = lax.rem(i, Y)
        side = jnp.where(i < Y, 1 - c, c)
        block = block_at(jnp.where(q < 2, q + 2, 3 - q))

        def put(k, value):
            part[side, block, k] = value

        lookup(block * C + side, L, rows, slots, weights, t2, oh, xs, put)

        @pl.when(i < Y)
        def _():
            to_sibling(q).start()

        @pl.when(i >= Y)
        def _():
            to_sibling(q).wait_recv()
            part[c, block] += from_core[q]

        @pl.when(i == 3)
        def _():
            for each in along_z:
                each.wait_recv()
            for each in along_y:
                each.start()
            to_core(0).start()

        @pl.when(i == Y)
        def _():
            for n in range(2):
                pack(part[c, block_at(2), half[n]], two_out.at[n])
                two_on[n].start()

    for each in along_y:
        each.wait_recv()
    for each in further:
        each.start()
    to_core(1).start()
    to_core(2).start()
    for n in range(2):
        two_on[n].wait_recv()
        add(block_at((1, 3)[n]), n, two_in.at[n])
        for m in range(2):
            pack(part[c, block_at((1, 3)[n]), half[m]], one_out.at[n, m])
        one_on[n].start()

    @pl.loop(0, 2 * Y)
    def _(i):
        k = lax.rem(i, 3)
        side = jnp.where((i < 3) | (i == 6), c, 1 - c)
        block = block_at(jnp.where(i >= 6, 2, jnp.where(k == 2, 3, k)))

        for n in range(3):

            @pl.when(i == 3 + n)
            def _():
                to_core(n).wait_recv()

        @pl.when(i == 5)
        def _():
            for each in further:
                each.wait_recv()
            to_core(3).start()

        @pl.when(i == 7)
        def _():
            to_core(3).wait_recv()

        gradient(block * C + side, L, lambda n: gall[side, block, n], rows, slots, weights, a, oh, acc)

        @pl.when(i == 4)
        def _():
            for n in range(2):
                one_on[n].wait_recv()
                for m in range(2):
                    add(y, m, one_in.at[n, m])
            for d in range(1, Z):
                pack(part[c, y, pl.ds(lax.rem(z + d, Z), 1)], z_out.at[d - 1])
                to_z(d).start()

    for h in range(H):
        v = acc[h * 64 : (h + 1) * 64, :]
        squares[x, h : h + 1, :] = jnp.sum(v * v, axis=0, keepdims=True)
    along_x = [
        copy(squares.at[x], squares.at[x], sx_s.at[d - 1], sx_r.at[d - 1], x_at(d)) for d in range(1, X)
    ]
    for each in along_x:
        each.start()

    for d in range(1, Z):
        to_z(d).wait_recv()
    total = part[c, y, z]
    for d in range(1, Z):
        total += unpack(z_in.at[d - 1], 1)[0]
    pooled[...] = total
    out = [pltpu.make_async_copy(pooled, pooled_out, store.at[0])]
    out[0].start()

    for each in along_x:
        each.wait_recv()
    norm = (squares[0] + squares[1]) + (squares[2] + squares[3])
    for h in range(H):
        cols = slice(h * L, (h + 1) * L)
        new = accum[:, cols] + norm[h : h + 1, :] / D
        new_accum[:, cols] = new
        moved = acc[h * 64 : (h + 1) * 64, :] * (STEP * lax.rsqrt(new))
        new_tab[:, cols] = (tab[:, cols].astype(F32) - moved).astype(BF)
    out += [
        pltpu.make_async_copy(new_tab, new_tab_out, store.at[1]),
        pltpu.make_async_copy(new_accum, new_accum_out, store.at[2]),
    ]
    out[1].start()
    out[2].start()

    for each in along_z + along_y + further + two_on + one_on + along_x:
        each.wait_send()
    for q in range(Y):
        to_core(q).wait_send()
        to_sibling(q).wait_send()
    for d in range(1, Z):
        to_z(d).wait_send()
    for each in out:
        each.wait()


def hand_on(*refs):
    n = (len(refs) - 2) // 3
    src, dst, held, come, go = refs[:n], refs[n : 2 * n], refs[2 * n : 3 * n], refs[-2], refs[-1]
    loads = [pltpu.make_async_copy(src[i], held[i], come.at[i]) for i in range(n)]
    stores = [pltpu.make_async_copy(held[i], dst[i], go.at[i]) for i in range(n)]
    for each in loads:
        each.start()
    for i in range(n):
        loads[i].wait()
        stores[i].start()
    for each in stores:
        each.wait()


def shards(table, accum, grad_pooled, sample_slot, row_slot, weight, send_count):
    _, dim, n_rows = table.shape
    own = grad_pooled.shape[2]
    L = n_rows // H
    half_rows = (Z // 2) * dim + 16
    dma = pltpu.SemaphoreType.DMA
    anywhere = pl.BlockSpec(memory_space=pl.ANY)
    shapes = (
        jax.ShapeDtypeStruct((dim, own), F32),
        jax.ShapeDtypeStruct((dim, n_rows), BF),
        jax.ShapeDtypeStruct((1, n_rows), F32),
    )
    results = pl.pallas_call(
        kernel,
        out_shape=shapes,
        in_specs=[anywhere] * 7,
        out_specs=(anywhere,) * 3,
        scratch_shapes=[pltpu.VMEM(each.shape, each.dtype) for each in shapes]
        + [dma((3,))]
        + [pltpu.VMEM((80, 128), F32)] * 3
        + [
            pltpu.VMEM((64 * H, L), BF),
            pltpu.VMEM((L, 1280), BF),
            pltpu.VMEM((64, 2048), BF),
            pltpu.VMEM((64 * H, 1280), BF),
            pltpu.VMEM((64 * H, L), F32),
            pltpu.VMEM((C, Y, Z, dim, own), BF),
            pltpu.VMEM((C, Y, Z, dim, own), F32),
            pltpu.VMEM((Y, Z, dim, own), F32),
            pltpu.VMEM((2, half_rows, own), jnp.int16),
            pltpu.VMEM((2, half_rows, own), jnp.int16),
            pltpu.VMEM((2, 2, half_rows, own), jnp.int16),
            pltpu.VMEM((2, 2, half_rows, own), jnp.int16),
            pltpu.VMEM((Z - 1, dim + 16, own), jnp.int16),
            pltpu.VMEM((Z - 1, dim + 16, own), jnp.int16),
            pltpu.VMEM((X, H, L), F32),
        ]
        + [pltpu.VMEM((dim, n_rows), BF), pltpu.VMEM((1, n_rows), F32)]
        + [pltpu.VMEM(sample_slot.shape[2:], jnp.int32)] * 3
        + [pltpu.VMEM(send_count.shape[1:], jnp.int32)]
        + [dma((n,)) for n in (7, 7, 7, 4, 4, 4, 4, 4, 4, 4, 4, 7, 7, 3, 3)],
        compiler_params=pltpu.CompilerParams(
            collective_id=0, has_side_effects=True, vmem_limit_bytes=64 << 20
        ),
    )(
        table[0],
        accum,
        grad_pooled[0],
        sample_slot[0, 0],
        row_slot[0, 0],
        weight[0, 0],
        send_count[0],
    )
    pooled, new_table, new_accum = pl.pallas_call(
        hand_on,
        out_shape=shapes,
        in_specs=[anywhere] * 3,
        out_specs=(anywhere,) * 3,
        scratch_shapes=[pltpu.VMEM(each.shape, each.dtype) for each in shapes] + [dma((3,)), dma((3,))],
        compiler_params=pltpu.CompilerParams(vmem_limit_bytes=64 << 20),
    )(*results)
    return pooled[None], new_table[None], new_accum


def solution(mesh):
    return jax.shard_map(
        shards,
        mesh=mesh,
        in_specs=(
            P(None, "dims", "rows"),
            P(None, "rows"),
            P(None, "dims", "rows"),
            P(None, "rows", None, None),
            P(None, "rows", None, None),
            P(None, "rows", None, None),
            P(None, "rows", None),
        ),
        out_specs=(P(None, "dims", "rows"), P(None, "dims", "rows"), P(None, "rows")),
        check_vma=False,
    )
```

```python
import jax
import jax.numpy as jnp
from jax import lax
from jax.experimental import pallas as pl
from jax.experimental.pallas import tpu as pltpu
from jax.sharding import PartitionSpec as P

D = 256
STEP = 0.3
H = 8
F32 = jnp.float32
BF = jnp.bfloat16
NT = (((1,), (1,)), ((), ()))
MESH = pl.DeviceIdType.MESH
Z, Y, C, X = 8, 4, 2, 4


def one():
    return jnp.ones((), BF)


def zero():
    return jnp.zeros((), BF)


def lay_out(row_ref, smp_ref, wgt_ref, cnt_ref, rows, slots, weights):
    eye = lax.broadcasted_iota(jnp.int32, (64, 64), 0) == lax.broadcasted_iota(jnp.int32, (64, 64), 1)
    count = jnp.where(eye, jnp.broadcast_to(cnt_ref[...], (64, 64)), 0).astype(F32)
    count = jnp.sum(count, axis=1, keepdims=True).astype(jnp.int32)
    lane = lax.broadcasted_iota(jnp.int32, (64, 128), 1)
    main = jnp.where(lane < count, wgt_ref[:, :128], 0)
    lane = lax.broadcasted_iota(jnp.int32, (64, 32), 1) + 128
    tail = jnp.where(lane < count, wgt_ref[:, 128:160], 0)
    for dst, m, t in (
        (rows, row_ref[:, :128], row_ref[:, 128:160]),
        (slots, smp_ref[:, :128], smp_ref[:, 128:160]),
        (weights, main, tail),
    ):
        dst[0:64, :] = m.astype(F32)
        t = t.astype(F32)
        for k in range(2):
            parts = [t[(4 * k + z) * 8 : (4 * k + z + 1) * 8, :] for z in range(4)]
            dst[64 + 8 * k : 72 + 8 * k, :] = jnp.concatenate(parts, axis=1)


def high_low(r, L):
    h = jnp.floor(r * (1.0 / L))
    return h, r - h * L


def lookup(s, L, rows, slots, weights, t2, oh, xs, put):
    iota = lax.broadcasted_iota(jnp.int32, (256, 128), 0).astype(F32).astype(BF)
    high = []
    for t in range(10):
        h, low = high_low(rows[pl.ds(t * 8 + s, 1), :], L)
        high.append(h)
        for k in range(L // 256):
            key = (low - 256.0 * k).astype(BF)
            oh[k * 256 : (k + 1) * 256, t * 128 : (t + 1) * 128] = jnp.where(iota == key, one(), zero())
    x2 = jnp.dot(t2[...], oh[...], preferred_element_type=F32)
    for t in range(10):
        cols = slice(t * 128, (t + 1) * 128)
        x = x2[0:64, cols]
        for h in range(1, H):
            x = jnp.where(high[t] == float(h), x2[h * 64 : (h + 1) * 64, cols], x)
        x = x.astype(BF)
        if t < 8:
            xs[:, t * 256 : t * 256 + 128] = x
        else:
            for z in range((t - 8) * 4, (t - 8) * 4 + 4):
                xs[:, z * 256 + 128 : z * 256 + 256] = x
    sample = lax.broadcasted_iota(jnp.int32, (128, 128), 0).astype(F32).astype(BF)
    lane = lax.broadcasted_iota(jnp.int32, (1, 128), 1)
    for z in range(8):
        at, tail = z * 8 + s, (8 + z // 4) * 8 + s
        mine = (lane >= 32 * (z % 4)) & (lane < 32 * (z % 4) + 32)
        tail_w = jnp.where(mine, weights[pl.ds(tail, 1), :], 0.0).astype(BF)
        spread = jnp.concatenate(
            [
                jnp.where(sample == slots[pl.ds(at, 1), :].astype(BF), weights[pl.ds(at, 1), :].astype(BF), zero()),
                jnp.where(sample == slots[pl.ds(tail, 1), :].astype(BF), tail_w, zero()),
            ],
            axis=1,
        )
        put(z, lax.dot_general(xs[:, z * 256 : (z + 1) * 256], spread, NT, preferred_element_type=F32))


def gradient(s, L, grad, rows, slots, weights, a, wr, acc):
    iota = lax.broadcasted_iota(jnp.int32, (256, 128), 0).astype(F32).astype(BF)
    lane = lax.broadcasted_iota(jnp.int32, (1, 128), 1)
    for t in range(10):
        cols = slice(t * 128, (t + 1) * 128)
        h, low = high_low(rows[pl.ds(t * 8 + s, 1), :], L)
        h = h.astype(BF)
        w = weights[pl.ds(t * 8 + s, 1), :].astype(BF)
        for k in range(L // 256):
            key = (low - 256.0 * k).astype(BF)
            wr[k * 256 : (k + 1) * 256, cols] = jnp.where(iota == key, w, zero())
        index = jnp.broadcast_to(slots[pl.ds(t * 8 + s, 1), :].astype(jnp.int32), (64, 128))

        def pick(z):
            return jnp.take_along_axis(grad(z).astype(F32), index, axis=1, mode="promise_in_bounds")

        if t < 8:
            e = pick(t)
        else:
            e = pick((t - 8) * 4)
            for z in range(1, 4):
                e = jnp.where(lane >= 32 * z, pick((t - 8) * 4 + z), e)
        e = e.astype(BF)
        for k in range(H):
            a[k * 64 : (k + 1) * 64, cols] = jnp.where(h == jnp.asarray(float(k), BF), e, zero())
    acc[...] += lax.dot_general(a[...], wr[...], NT, preferred_element_type=F32)


def pack(values, dst):
    n, dim, own = values.shape
    row = lax.broadcasted_iota(jnp.int32, (16, own), 0)
    exponents = jnp.zeros((16, own), F32)
    for j in range(n):
        top = jnp.max(jnp.abs(values[j]), axis=0, keepdims=True)
        e = jnp.ceil(jnp.log2(jnp.maximum(top, 1e-30)))
        dst[j * dim : (j + 1) * dim, :] = jnp.round(values[j] * jnp.exp2(14.0 - e)).astype(jnp.int32).astype(jnp.int16)
        exponents = jnp.where(row == j, e, exponents)
    dst[n * dim : n * dim + 16, :] = exponents.astype(jnp.int32).astype(jnp.int16)


def unpack(src, n):
    dim = (src.shape[0] - 16) // n
    exponents = src[n * dim : n * dim + 16, :].astype(jnp.int32).astype(F32)
    return [
        src[j * dim : (j + 1) * dim, :].astype(jnp.int32).astype(F32) * jnp.exp2(exponents[j : j + 1, :] - 14.0)
        for j in range(n)
    ]


def kernel(
    tab_in, accum_in, g, smp_in, row_in, wgt_in, cnt_in,
    pooled_out, new_tab_out, new_accum_out,
    pooled, new_tab, new_accum, store, rows, slots, weights, t2, oh, xs, a, acc,
    gall, part, from_core, two_out, two_in, one_out, one_in, z_out, z_in, squares,
    tab, accum, smp, row, wgt, cnt, load, gz_s, gz_r, gy_s, gy_r, gc_s, gc_r, pc_s, pc_r, py_s, py_r, pz_s, pz_r, sx_s, sx_r,
):
    L = tab.shape[1] // H
    pairs = ((cnt_in, cnt), (wgt_in, wgt), (row_in, row), (smp_in, smp), (tab_in, tab), (accum_in, accum))
    loads = [pltpu.make_async_copy(src, dst, load.at[i]) for i, (src, dst) in enumerate(pairs)]
    for each in loads:
        each.start()
    r, x = lax.axis_index("rows"), lax.axis_index("dims")
    z, y, c = r // (Y * C), lax.rem(r // C, Y), lax.rem(r, C)

    def z_at(d):
        return (lax.rem(z + d, Z) * (Y * C) + y * C + c, x)

    def y_at(d):
        return (z * (Y * C) + lax.rem(y + d, Y) * C + c, x)

    def x_at(d):
        return (r, lax.rem(x + d, X))

    sibling = (z * (Y * C) + y * C + (1 - c), x)

    def copy(src, dst, send, recv, to):
        return pltpu.make_async_remote_copy(
            src_ref=src, dst_ref=dst, send_sem=send, recv_sem=recv, device_id=to, device_id_type=MESH
        )

    barrier = pltpu.get_barrier_semaphore()
    peers = [z_at(d) for d in range(1, Z)] + [y_at(d) for d in range(1, Y)] + [sibling]
    peers += [x_at(d) for d in range(1, X)]
    for to in peers:
        pl.semaphore_signal(barrier, inc=1, device_id=to, device_id_type=MESH)

    own_grad = pltpu.make_async_copy(g, gall.at[c, y, z], load.at[len(pairs)])
    own_grad.start()
    acc[...] = jnp.zeros_like(acc)
    own_grad.wait()
    pl.semaphore_wait(barrier, len(peers))

    along_z = [
        copy(gall.at[c, y, z], gall.at[c, y, z], gz_s.at[d - 1], gz_r.at[d - 1], z_at(d)) for d in range(1, Z)
    ]

    def block_at(d):
        return lax.rem(y + d, Y)

    half = (pl.ds(0, Z // 2), pl.ds(Z // 2, Z // 2))
    def along_y(e):
        at = lax.rem(z + e, Z)
        return [
            copy(gall.at[c, y, at], gall.at[c, y, at], gy_s.at[2 + n, e], gy_r.at[2 + n, e], y_at((1, 3)[n]))
            for n in range(2)
        ]

    near, far = (0, 1, 2, 6, 7), (3, 4, 5)
    further = [
        copy(gall.at[c, block_at(3), half[0]], gall.at[c, block_at(3), half[0]], gy_s.at[0, 0], gy_r.at[0, 0], y_at(1)),
        copy(gall.at[c, block_at(1), half[1]], gall.at[c, block_at(1), half[1]], gy_s.at[1, 0], gy_r.at[1, 0], y_at(3)),
    ]

    def to_core(k):
        block = block_at((0, 1, 3, 2)[k])
        return copy(gall.at[c, block], gall.at[c, block], gc_s.at[k], gc_r.at[k], sibling)

    for each in along_z:
        each.start()

    for each in loads:
        each.wait()
    lay_out(row, smp, wgt, cnt, rows, slots, weights)
    for h in range(H):
        t2[h * 64 : (h + 1) * 64, :] = tab[:, h * L : (h + 1) * L]

    def order(q):
        return block_at(jnp.where(q < 2, 2 - q, jnp.where(q == 2, 3, 0)))

    def to_sibling(q):
        block = order(q)
        return copy(part.at[1 - c, block], from_core.at[q], pc_s.at[q], pc_r.at[q], sibling)

    two_on = [
        copy(two_out.at[0], two_in.at[0], py_s.at[0], py_r.at[0], y_at(2)),
        copy(two_out.at[1], two_in.at[1], py_s.at[1], py_r.at[1], y_at(3)),
    ]
    one_on = [copy(one_out.at[n], one_in.at[n], py_s.at[2 + n], py_r.at[2 + n], y_at((1, 3)[n])) for n in range(2)]

    def add(block, n, packed):
        values = unpack(packed, Z // 2)
        for j in range(Z // 2):
            part[c, block, n * (Z // 2) + j] += values[j]

    def to_z(d):
        return copy(z_out.at[d - 1], z_in.at[d - 1], pz_s.at[d - 1], pz_r.at[d - 1], z_at(d))

    def look(q, side, n):
        block = order(q)

        def put(k, value):
            part[side, block, k] = value

        lookup(block * C + side, L, rows, slots, weights, t2, oh.at[n], xs.at[n], put)

    def add_core(q):
        to_sibling(q).wait_recv()
        part[c, order(q)] += from_core[q]

    look(0, 1 - c, 0)
    to_sibling(0).start()

    @pl.loop(0, Y - 1)
    def _(q):
        look(q, c, 1)
        look(q + 1, 1 - c, 0)
        to_sibling(q + 1).start()
        add_core(q)

        @pl.when(q == 0)
        def _():
            for n in range(2):
                pack(part[c, block_at(2), half[n]], two_out.at[n])
                two_on[n].start()
            for e in near:
                if e > 0:
                    along_z[Z - e - 1].wait_recv()
                for each in along_y(e):
                    each.start()

        @pl.when(q == 1)
        def _():
            for e in far:
                along_z[Z - e - 1].wait_recv()
                for each in along_y(e):
                    each.start()
            for m in range(2):
                pack(part[c, block_at(1), half[m]], one_out.at[0, m])
            one_on[0].start()
            to_core(0).start()

        @pl.when(q == 2)
        def _():
            two_on[1].wait_recv()
            add(block_at(3), 1, two_in.at[1])
            for m in range(2):
                pack(part[c, block_at(3), half[m]], one_out.at[1, m])
            one_on[1].start()

    look(Y - 1, c, 1)
    for e in near + far:
        for each in along_y(e):
            each.wait_recv()
    for each in further:
        each.start()
    to_core(1).start()
    to_core(2).start()
    add_core(Y - 1)
    to_core(0).wait_recv()

    @pl.loop(0, Y)
    def _(i):

        @pl.when(i == 2)
        def _():
            to_core(1).wait_recv()
            to_core(2).wait_recv()
            for each in further:
                each.wait_recv()
            to_core(3).start()

        @pl.when(i == 3)
        def _():
            to_core(3).wait_recv()

        for n in range(2):
            middle = (i == 1) | (i == 2)
            side = jnp.where(middle, jnp.where(i == 1, c, 1 - c), c if n == 0 else 1 - c)
            block = block_at(jnp.where(middle, 1 if n == 0 else 3, jnp.where(i == 0, 0, 2)))

            def grad(k, side=side, block=block):
                return gall[side, block, k]

            gradient(block * C + side, L, grad, rows, slots, weights, a.at[n], oh.at[n], acc)

        @pl.when(i == 1)
        def _():
            two_on[0].wait_recv()
            add(y, 0, two_in.at[0])
            for n in range(2):
                one_on[n].wait_recv()
                for m in range(2):
                    add(y, m, one_in.at[n, m])
            for d in range(1, Z):
                pack(part[c, y, pl.ds(lax.rem(z + d, Z), 1)], z_out.at[d - 1])
                to_z(d).start()

    for h in range(H):
        v = acc[h * 64 : (h + 1) * 64, :]
        squares[x, h : h + 1, :] = jnp.sum(v * v, axis=0, keepdims=True)
    along_x = [
        copy(squares.at[x], squares.at[x], sx_s.at[d - 1], sx_r.at[d - 1], x_at(d)) for d in range(1, X)
    ]
    for each in along_x:
        each.start()

    for d in range(1, Z):
        to_z(d).wait_recv()
    total = part[c, y, z]
    for d in range(1, Z):
        total += unpack(z_in.at[d - 1], 1)[0]
    pooled[...] = total
    out = [pltpu.make_async_copy(pooled, pooled_out, store.at[0])]
    out[0].start()

    for each in along_x:
        each.wait_recv()
    norm = (squares[0] + squares[1]) + (squares[2] + squares[3])
    for h in range(H):
        cols = slice(h * L, (h + 1) * L)
        new = accum[:, cols] + norm[h : h + 1, :] / D
        new_accum[:, cols] = new
        moved = acc[h * 64 : (h + 1) * 64, :] * (STEP * lax.rsqrt(new))
        new_tab[:, cols] = (tab[:, cols].astype(F32) - moved).astype(BF)
    out += [
        pltpu.make_async_copy(new_tab, new_tab_out, store.at[1]),
        pltpu.make_async_copy(new_accum, new_accum_out, store.at[2]),
    ]
    out[1].start()
    out[2].start()

    for each in along_z + further + two_on + one_on + along_x:
        each.wait_send()
    for e in range(Z):
        for each in along_y(e):
            each.wait_send()
    for q in range(Y):
        to_core(q).wait_send()
        to_sibling(q).wait_send()
    for d in range(1, Z):
        to_z(d).wait_send()
    for each in out:
        each.wait()


def hand_on(*refs):
    n = (len(refs) - 2) // 3
    src, dst, held, come, go = refs[:n], refs[n : 2 * n], refs[2 * n : 3 * n], refs[-2], refs[-1]
    loads = [pltpu.make_async_copy(src[i], held[i], come.at[i]) for i in range(n)]
    stores = [pltpu.make_async_copy(held[i], dst[i], go.at[i]) for i in range(n)]
    for each in loads:
        each.start()
    for i in range(n):
        loads[i].wait()
        stores[i].start()
    for each in stores:
        each.wait()


def shards(table, accum, grad_pooled, sample_slot, row_slot, weight, send_count):
    _, dim, n_rows = table.shape
    own = grad_pooled.shape[2]
    L = n_rows // H
    half_rows = (Z // 2) * dim + 16
    dma = pltpu.SemaphoreType.DMA
    anywhere = pl.BlockSpec(memory_space=pl.ANY)
    shapes = (
        jax.ShapeDtypeStruct((dim, own), F32),
        jax.ShapeDtypeStruct((dim, n_rows), BF),
        jax.ShapeDtypeStruct((1, n_rows), F32),
    )
    results = pl.pallas_call(
        kernel,
        out_shape=shapes,
        in_specs=[anywhere] * 7,
        out_specs=(anywhere,) * 3,
        scratch_shapes=[pltpu.VMEM(each.shape, each.dtype) for each in shapes]
        + [dma((3,))]
        + [pltpu.VMEM((80, 128), F32)] * 3
        + [
            pltpu.VMEM((64 * H, L), BF),
            pltpu.VMEM((2, L, 1280), BF),
            pltpu.VMEM((2, 64, 2048), BF),
            pltpu.VMEM((2, 64 * H, 1280), BF),
            pltpu.VMEM((64 * H, L), F32),
            pltpu.VMEM((C, Y, Z, dim, own), BF),
            pltpu.VMEM((C, Y, Z, dim, own), F32),
            pltpu.VMEM((Y, Z, dim, own), F32),
            pltpu.VMEM((2, half_rows, own), jnp.int16),
            pltpu.VMEM((2, half_rows, own), jnp.int16),
            pltpu.VMEM((2, 2, half_rows, own), jnp.int16),
            pltpu.VMEM((2, 2, half_rows, own), jnp.int16),
            pltpu.VMEM((Z - 1, dim + 16, own), jnp.int16),
            pltpu.VMEM((Z - 1, dim + 16, own), jnp.int16),
            pltpu.VMEM((X, H, L), F32),
        ]
        + [pltpu.VMEM((dim, n_rows), BF), pltpu.VMEM((1, n_rows), F32)]
        + [pltpu.VMEM(sample_slot.shape[2:], jnp.int32)] * 3
        + [pltpu.VMEM(send_count.shape[1:], jnp.int32)]
        + [dma((n,)) for n in (7, 7, 7)]
        + [dma((4, Z)), dma((4, Z))]
        + [dma((n,)) for n in (4, 4, 4, 4, 4, 4, 7, 7, 3, 3)],
        compiler_params=pltpu.CompilerParams(
            collective_id=0, has_side_effects=True, vmem_limit_bytes=64 << 20
        ),
    )(
        table[0],
        accum,
        grad_pooled[0],
        sample_slot[0, 0],
        row_slot[0, 0],
        weight[0, 0],
        send_count[0],
    )
    pooled, new_table, new_accum = pl.pallas_call(
        hand_on,
        out_shape=shapes,
        in_specs=[anywhere] * 3,
        out_specs=(anywhere,) * 3,
        scratch_shapes=[pltpu.VMEM(each.shape, each.dtype) for each in shapes] + [dma((3,)), dma((3,))],
        compiler_params=pltpu.CompilerParams(vmem_limit_bytes=64 << 20),
    )(*results)
    return pooled[None], new_table[None], new_accum


def solution(mesh):
    return jax.shard_map(
        shards,
        mesh=mesh,
        in_specs=(
            P(None, "dims", "rows"),
            P(None, "rows"),
            P(None, "dims", "rows"),
            P(None, "rows", None, None),
            P(None, "rows", None, None),
            P(None, "rows", None, None),
            P(None, "rows", None),
        ),
        out_specs=(P(None, "dims", "rows"), P(None, "dims", "rows"), P(None, "rows")),
        check_vma=False,
    )
```

```python
import jax
import jax.numpy as jnp
from jax import lax
from jax.experimental import pallas as pl
from jax.experimental.pallas import tpu as pltpu
from jax.sharding import PartitionSpec as P

D = 256
STEP = 0.3
H = 8
F32 = jnp.float32
BF = jnp.bfloat16
NT = (((1,), (1,)), ((), ()))
MESH = pl.DeviceIdType.MESH
Z, Y, C, X = 8, 4, 2, 4


def one():
    return jnp.ones((), BF)


def zero():
    return jnp.zeros((), BF)


def lay_out(row_ref, smp_ref, wgt_ref, cnt_ref, rows, slots, weights):
    eye = lax.broadcasted_iota(jnp.int32, (64, 64), 0) == lax.broadcasted_iota(jnp.int32, (64, 64), 1)
    count = jnp.where(eye, jnp.broadcast_to(cnt_ref[...], (64, 64)), 0).astype(F32)
    count = jnp.sum(count, axis=1, keepdims=True).astype(jnp.int32)
    lane = lax.broadcasted_iota(jnp.int32, (64, 128), 1)
    main = jnp.where(lane < count, wgt_ref[:, :128], 0)
    lane = lax.broadcasted_iota(jnp.int32, (64, 32), 1) + 128
    tail = jnp.where(lane < count, wgt_ref[:, 128:160], 0)
    for dst, m, t in (
        (rows, row_ref[:, :128], row_ref[:, 128:160]),
        (slots, smp_ref[:, :128], smp_ref[:, 128:160]),
        (weights, main, tail),
    ):
        dst[0:64, :] = m.astype(F32)
        t = t.astype(F32)
        for k in range(2):
            parts = [t[(4 * k + z) * 8 : (4 * k + z + 1) * 8, :] for z in range(4)]
            dst[64 + 8 * k : 72 + 8 * k, :] = jnp.concatenate(parts, axis=1)


def high_low(r, L):
    h = jnp.floor(r * (1.0 / L))
    return h, r - h * L


def lookup(s, L, rows, slots, weights, t2, oh, xs, put):
    iota = lax.broadcasted_iota(jnp.int32, (256, 128), 0).astype(F32).astype(BF)
    high = []
    for t in range(10):
        h, low = high_low(rows[pl.ds(t * 8 + s, 1), :], L)
        high.append(h)
        for k in range(L // 256):
            key = (low - 256.0 * k).astype(BF)
            oh[k * 256 : (k + 1) * 256, t * 128 : (t + 1) * 128] = jnp.where(iota == key, one(), zero())
    x2 = jnp.dot(t2[...], oh[...], preferred_element_type=F32)
    for t in range(10):
        cols = slice(t * 128, (t + 1) * 128)
        x = x2[0:64, cols]
        for h in range(1, H):
            x = jnp.where(high[t] == float(h), x2[h * 64 : (h + 1) * 64, cols], x)
        x = x.astype(BF)
        if t < 8:
            xs[:, t * 256 : t * 256 + 128] = x
        else:
            for z in range((t - 8) * 4, (t - 8) * 4 + 4):
                xs[:, z * 256 + 128 : z * 256 + 256] = x
    sample = lax.broadcasted_iota(jnp.int32, (128, 128), 0).astype(F32).astype(BF)
    lane = lax.broadcasted_iota(jnp.int32, (1, 128), 1)
    for z in range(8):
        at, tail = z * 8 + s, (8 + z // 4) * 8 + s
        mine = (lane >= 32 * (z % 4)) & (lane < 32 * (z % 4) + 32)
        tail_w = jnp.where(mine, weights[pl.ds(tail, 1), :], 0.0).astype(BF)
        spread = jnp.concatenate(
            [
                jnp.where(sample == slots[pl.ds(at, 1), :].astype(BF), weights[pl.ds(at, 1), :].astype(BF), zero()),
                jnp.where(sample == slots[pl.ds(tail, 1), :].astype(BF), tail_w, zero()),
            ],
            axis=1,
        )
        put(z, lax.dot_general(xs[:, z * 256 : (z + 1) * 256], spread, NT, preferred_element_type=F32))


def gradient(s, L, grad, rows, slots, weights, a, wr, acc):
    iota = lax.broadcasted_iota(jnp.int32, (256, 128), 0).astype(F32).astype(BF)
    lane = lax.broadcasted_iota(jnp.int32, (1, 128), 1)
    for t in range(10):
        cols = slice(t * 128, (t + 1) * 128)
        h, low = high_low(rows[pl.ds(t * 8 + s, 1), :], L)
        h = h.astype(BF)
        w = weights[pl.ds(t * 8 + s, 1), :].astype(BF)
        for k in range(L // 256):
            key = (low - 256.0 * k).astype(BF)
            wr[k * 256 : (k + 1) * 256, cols] = jnp.where(iota == key, w, zero())
        index = jnp.broadcast_to(slots[pl.ds(t * 8 + s, 1), :].astype(jnp.int32), (64, 128))

        def pick(z):
            return jnp.take_along_axis(grad(z).astype(F32), index, axis=1, mode="promise_in_bounds")

        if t < 8:
            e = pick(t)
        else:
            e = pick((t - 8) * 4)
            for z in range(1, 4):
                e = jnp.where(lane >= 32 * z, pick((t - 8) * 4 + z), e)
        e = e.astype(BF)
        for k in range(H):
            a[k * 64 : (k + 1) * 64, cols] = jnp.where(h == jnp.asarray(float(k), BF), e, zero())
    acc[...] += lax.dot_general(a[...], wr[...], NT, preferred_element_type=F32)


def pack(values, dst):
    n, dim, own = values.shape
    row = lax.broadcasted_iota(jnp.int32, (16, own), 0)
    exponents = jnp.zeros((16, own), F32)
    for j in range(n):
        top = jnp.max(jnp.abs(values[j]), axis=0, keepdims=True)
        e = jnp.ceil(jnp.log2(jnp.maximum(top, 1e-30)))
        dst[j * dim : (j + 1) * dim, :] = jnp.round(values[j] * jnp.exp2(14.0 - e)).astype(jnp.int32).astype(jnp.int16)
        exponents = jnp.where(row == j, e, exponents)
    dst[n * dim : n * dim + 16, :] = exponents.astype(jnp.int32).astype(jnp.int16)


def unpack(src, n):
    dim = (src.shape[0] - 16) // n
    exponents = src[n * dim : n * dim + 16, :].astype(jnp.int32).astype(F32)
    return [
        src[j * dim : (j + 1) * dim, :].astype(jnp.int32).astype(F32) * jnp.exp2(exponents[j : j + 1, :] - 14.0)
        for j in range(n)
    ]


def kernel(
    tab_in, accum_in, g, smp_in, row_in, wgt_in, cnt_in,
    pooled_out, new_tab_out, new_accum_out,
    pooled, new_tab, new_accum, store, rows, slots, weights, t2, oh, xs, a, acc,
    gall, part, from_core, two_out, two_in, one_out, one_in, z_out, z_in, squares,
    tab, accum, smp, row, wgt, cnt, load, gz_s, gz_r, gy_s, gy_r, gc_s, gc_r, pc_s, pc_r, py_s, py_r, pz_s, pz_r, sx_s, sx_r,
):
    L = tab.shape[1] // H
    pairs = ((cnt_in, cnt), (wgt_in, wgt), (row_in, row), (smp_in, smp), (tab_in, tab), (accum_in, accum))
    loads = [pltpu.make_async_copy(src, dst, load.at[i]) for i, (src, dst) in enumerate(pairs)]
    r, x = lax.axis_index("rows"), lax.axis_index("dims")
    z, y, c = r // (Y * C), lax.rem(r // C, Y), lax.rem(r, C)

    own_grad = pltpu.make_async_copy(g, gall.at[c, y, z], load.at[len(pairs)])
    own_grad.start()
    for each in loads:
        each.start()

    def z_at(d):
        return (lax.rem(z + d, Z) * (Y * C) + y * C + c, x)

    def y_at(d):
        return (z * (Y * C) + lax.rem(y + d, Y) * C + c, x)

    def x_at(d):
        return (r, lax.rem(x + d, X))

    sibling = (z * (Y * C) + y * C + (1 - c), x)

    def copy(src, dst, send, recv, to):
        return pltpu.make_async_remote_copy(
            src_ref=src, dst_ref=dst, send_sem=send, recv_sem=recv, device_id=to, device_id_type=MESH
        )

    barrier = pltpu.get_barrier_semaphore()
    peers = [z_at(d) for d in range(1, Z)] + [y_at(d) for d in range(1, Y)] + [sibling]
    peers += [x_at(d) for d in range(1, X)]
    for to in peers:
        pl.semaphore_signal(barrier, inc=1, device_id=to, device_id_type=MESH)

    acc[...] = jnp.zeros_like(acc)
    own_grad.wait()
    pl.semaphore_wait(barrier, len(peers))

    along_z = [
        copy(gall.at[c, y, z], gall.at[c, y, z], gz_s.at[d - 1], gz_r.at[d - 1], z_at(d)) for d in range(1, Z)
    ]

    def block_at(d):
        return lax.rem(y + d, Y)

    half = (pl.ds(0, Z // 2), pl.ds(Z // 2, Z // 2))
    def along_y(e):
        at = lax.rem(z + e, Z)
        return [
            copy(gall.at[c, y, at], gall.at[c, y, at], gy_s.at[1 + n, e], gy_r.at[1 + n, e], y_at((1, 3)[n]))
            for n in range(2)
        ]

    near, far = (0, 1, 2, 6, 7), (3, 4, 5)
    def further(e):
        at = lax.rem(z + e, Z)
        up = e in (0, 1, 6, 3)
        block = block_at(3 if up else 1)
        return copy(gall.at[c, block, at], gall.at[c, block, at], gy_s.at[0, e], gy_r.at[0, e], y_at(1 if up else 3))

    def to_core(k):
        block = block_at((0, 1, 3, 2)[k])
        return copy(gall.at[c, block], gall.at[c, block], gc_s.at[k], gc_r.at[k], sibling)

    for each in along_z:
        each.start()

    for each in loads:
        each.wait()
    lay_out(row, smp, wgt, cnt, rows, slots, weights)
    for h in range(H):
        t2[h * 64 : (h + 1) * 64, :] = tab[:, h * L : (h + 1) * L]

    def order(q):
        return block_at(jnp.where(q < 2, 2 - q, jnp.where(q == 2, 3, 0)))

    def to_sibling(q):
        block = order(q)
        return copy(part.at[1 - c, block], from_core.at[q], pc_s.at[q], pc_r.at[q], sibling)

    two_on = [
        copy(two_out.at[0], two_in.at[0], py_s.at[0], py_r.at[0], y_at(2)),
        copy(two_out.at[1], two_in.at[1], py_s.at[1], py_r.at[1], y_at(3)),
    ]
    one_on = [copy(one_out.at[n], one_in.at[n], py_s.at[2 + n], py_r.at[2 + n], y_at((1, 3)[n])) for n in range(2)]

    def add(block, n, packed):
        values = unpack(packed, Z // 2)
        for j in range(Z // 2):
            part[c, block, n * (Z // 2) + j] += values[j]

    def to_z(d):
        return copy(z_out.at[d - 1], z_in.at[d - 1], pz_s.at[d - 1], pz_r.at[d - 1], z_at(d))

    def look(q, side, n):
        block = order(q)

        def put(k, value):
            part[side, block, k] = value

        lookup(block * C + side, L, rows, slots, weights, t2, oh.at[n], xs.at[n], put)

    def add_core(q):
        to_sibling(q).wait_recv()
        part[c, order(q)] += from_core[q]

    look(0, 1 - c, 0)
    to_sibling(0).start()

    @pl.loop(0, Y - 1)
    def _(q):
        look(q, c, 1)
        look(q + 1, 1 - c, 0)
        to_sibling(q + 1).start()
        add_core(q)

        @pl.when(q == 0)
        def _():
            for e in near:
                if e > 0:
                    along_z[Z - e - 1].wait_recv()
                for each in along_y(e):
                    each.start()
            for n in (1, 0):
                pack(part[c, block_at(2), half[n]], two_out.at[n])
                two_on[n].start()

        @pl.when(q == 1)
        def _():
            for e in far:
                along_z[Z - e - 1].wait_recv()
                for each in along_y(e):
                    each.start()
            for m in range(2):
                pack(part[c, block_at(1), half[m]], one_out.at[0, m])
            one_on[0].start()
            to_core(0).start()

        @pl.when(q == 2)
        def _():
            for e in near:
                for each in along_y(e):
                    each.wait_recv()
                further(e).start()
            two_on[1].wait_recv()
            add(block_at(3), 1, two_in.at[1])
            for m in range(2):
                pack(part[c, block_at(3), half[m]], one_out.at[1, m])
            one_on[1].start()

    def grad_of(side, d, n):
        block = block_at(d)

        def grad(k):
            return gall[side, block, k]

        gradient(block * C + side, L, grad, rows, slots, weights, a.at[n], oh.at[n], acc)

    look(Y - 1, c, 1)
    grad_of(c, 0, 0)
    for e in far:
        for each in along_y(e):
            each.wait_recv()
        further(e).start()
    to_core(1).start()
    to_core(2).start()
    add_core(Y - 1)
    to_core(0).wait_recv()

    @pl.loop(0, Y - 1)
    def _(i):

        @pl.when(i == 1)
        def _():
            to_core(1).wait_recv()

        @pl.when(i == 2)
        def _():
            for e in range(Z):
                further(e).wait_recv()
            to_core(3).start()
            to_core(2).wait_recv()

        grad_of(jnp.where(i == 1, c, 1 - c), jnp.where(i == 0, 0, 3), 0)
        grad_of(jnp.where(i == 1, 1 - c, c), jnp.where(i == 2, 2, 1), 1)

        @pl.when(i == 1)
        def _():
            two_on[0].wait_recv()
            add(y, 0, two_in.at[0])
            for n in range(2):
                one_on[n].wait_recv()
                for m in range(2):
                    add(y, m, one_in.at[n, m])
            for d in range(1, Z):
                pack(part[c, y, pl.ds(lax.rem(z + d, Z), 1)], z_out.at[d - 1])
                to_z(d).start()

    to_core(3).wait_recv()
    grad_of(1 - c, 2, 0)

    for h in range(H):
        v = acc[h * 64 : (h + 1) * 64, :]
        squares[x, h : h + 1, :] = jnp.sum(v * v, axis=0, keepdims=True)
    along_x = [
        copy(squares.at[x], squares.at[x], sx_s.at[d - 1], sx_r.at[d - 1], x_at(d)) for d in range(1, X)
    ]
    for each in along_x:
        each.start()

    for d in range(1, Z):
        to_z(d).wait_recv()
    total = part[c, y, z]
    for d in range(1, Z):
        total += unpack(z_in.at[d - 1], 1)[0]
    pooled[...] = total
    out = [pltpu.make_async_copy(pooled, pooled_out, store.at[0])]
    out[0].start()

    for each in along_x:
        each.wait_recv()
    norm = (squares[0] + squares[1]) + (squares[2] + squares[3])
    for h in range(H):
        cols = slice(h * L, (h + 1) * L)
        new = accum[:, cols] + norm[h : h + 1, :] / D
        new_accum[:, cols] = new
        moved = acc[h * 64 : (h + 1) * 64, :] * (STEP * lax.rsqrt(new))
        new_tab[:, cols] = (tab[:, cols].astype(F32) - moved).astype(BF)
        if h % 2 == 1:
            cols = pl.ds((h - 1) * L, 2 * L)
            out.append(pltpu.make_async_copy(new_tab.at[:, cols], new_tab_out.at[:, cols], store.at[2 + h // 2]))
            out[-1].start()
    out.append(pltpu.make_async_copy(new_accum, new_accum_out, store.at[1]))
    out[-1].start()

    for each in along_z + two_on + one_on + along_x:
        each.wait_send()
    for e in range(Z):
        further(e).wait_send()
        for each in along_y(e):
            each.wait_send()
    for q in range(Y):
        to_core(q).wait_send()
        to_sibling(q).wait_send()
    for d in range(1, Z):
        to_z(d).wait_send()
    for each in out:
        each.wait()


def hand_on(*refs):
    n = (len(refs) - 2) // 3
    src, dst, held, come, go = refs[:n], refs[n : 2 * n], refs[2 * n : 3 * n], refs[-2], refs[-1]
    pieces = [(src[1].at[rows], held[1].at[rows], dst[1].at[rows]) for rows in [pl.ds(16 * k, 16) for k in range(4)]]
    pieces += [(src[i], held[i], dst[i]) for i in (0, 2)]
    loads = [pltpu.make_async_copy(p[0], p[1], come.at[i]) for i, p in enumerate(pieces)]
    stores = [pltpu.make_async_copy(p[1], p[2], go.at[i]) for i, p in enumerate(pieces)]
    for each in loads:
        each.start()
    for load, store in zip(loads, stores):
        load.wait()
        store.start()
    for each in stores:
        each.wait()


def shards(table, accum, grad_pooled, sample_slot, row_slot, weight, send_count):
    _, dim, n_rows = table.shape
    own = grad_pooled.shape[2]
    L = n_rows // H
    half_rows = (Z // 2) * dim + 16
    dma = pltpu.SemaphoreType.DMA
    anywhere = pl.BlockSpec(memory_space=pl.ANY)
    shapes = (
        jax.ShapeDtypeStruct((dim, own), F32),
        jax.ShapeDtypeStruct((dim, n_rows), BF),
        jax.ShapeDtypeStruct((1, n_rows), F32),
    )
    results = pl.pallas_call(
        kernel,
        out_shape=shapes,
        in_specs=[anywhere] * 7,
        out_specs=(anywhere,) * 3,
        scratch_shapes=[pltpu.VMEM(each.shape, each.dtype) for each in shapes]
        + [dma((2 + H // 2,))]
        + [pltpu.VMEM((80, 128), F32)] * 3
        + [
            pltpu.VMEM((64 * H, L), BF),
            pltpu.VMEM((2, L, 1280), BF),
            pltpu.VMEM((2, 64, 2048), BF),
            pltpu.VMEM((2, 64 * H, 1280), BF),
            pltpu.VMEM((64 * H, L), F32),
            pltpu.VMEM((C, Y, Z, dim, own), BF),
            pltpu.VMEM((C, Y, Z, dim, own), F32),
            pltpu.VMEM((Y, Z, dim, own), F32),
            pltpu.VMEM((2, half_rows, own), jnp.int16),
            pltpu.VMEM((2, half_rows, own), jnp.int16),
            pltpu.VMEM((2, 2, half_rows, own), jnp.int16),
            pltpu.VMEM((2, 2, half_rows, own), jnp.int16),
            pltpu.VMEM((Z - 1, dim + 16, own), jnp.int16),
            pltpu.VMEM((Z - 1, dim + 16, own), jnp.int16),
            pltpu.VMEM((X, H, L), F32),
        ]
        + [pltpu.VMEM((dim, n_rows), BF), pltpu.VMEM((1, n_rows), F32)]
        + [pltpu.VMEM(sample_slot.shape[2:], jnp.int32)] * 3
        + [pltpu.VMEM(send_count.shape[1:], jnp.int32)]
        + [dma((n,)) for n in (7, 7, 7)]
        + [dma((3, Z)), dma((3, Z))]
        + [dma((n,)) for n in (4, 4, 4, 4, 4, 4, 7, 7, 3, 3)],
        compiler_params=pltpu.CompilerParams(
            collective_id=0, has_side_effects=True, vmem_limit_bytes=64 << 20
        ),
    )(
        table[0],
        accum,
        grad_pooled[0],
        sample_slot[0, 0],
        row_slot[0, 0],
        weight[0, 0],
        send_count[0],
    )
    pooled, new_table, new_accum = pl.pallas_call(
        hand_on,
        out_shape=shapes,
        in_specs=[anywhere] * 3,
        out_specs=(anywhere,) * 3,
        scratch_shapes=[pltpu.VMEM(each.shape, each.dtype) for each in shapes] + [dma((6,)), dma((6,))],
        compiler_params=pltpu.CompilerParams(vmem_limit_bytes=64 << 20),
    )(*results)
    return pooled[None], new_table[None], new_accum


def solution(mesh):
    return jax.shard_map(
        shards,
        mesh=mesh,
        in_specs=(
            P(None, "dims", "rows"),
            P(None, "rows"),
            P(None, "dims", "rows"),
            P(None, "rows", None, None),
            P(None, "rows", None, None),
            P(None, "rows", None, None),
            P(None, "rows", None),
        ),
        out_specs=(P(None, "dims", "rows"), P(None, "dims", "rows"), P(None, "rows")),
        check_vma=False,
    )
```

```python
import jax
import jax.numpy as jnp
from jax import lax
from jax.experimental import pallas as pl
from jax.experimental.pallas import tpu as pltpu
from jax.sharding import PartitionSpec as P

D = 256
STEP = 0.3
H = 8
F32 = jnp.float32
BF = jnp.bfloat16
NT = (((1,), (1,)), ((), ()))
MESH = pl.DeviceIdType.MESH
Z, Y, C, X = 8, 4, 2, 4


def one():
    return jnp.ones((), BF)


def zero():
    return jnp.zeros((), BF)


def lay_out(row_ref, smp_ref, wgt_ref, cnt_ref, rows, slots, weights):
    eye = lax.broadcasted_iota(jnp.int32, (64, 64), 0) == lax.broadcasted_iota(jnp.int32, (64, 64), 1)
    count = jnp.where(eye, jnp.broadcast_to(cnt_ref[...], (64, 64)), 0).astype(F32)
    count = jnp.sum(count, axis=1, keepdims=True).astype(jnp.int32)
    lane = lax.broadcasted_iota(jnp.int32, (64, 128), 1)
    main = jnp.where(lane < count, wgt_ref[:, :128], 0)
    lane = lax.broadcasted_iota(jnp.int32, (64, 32), 1) + 128
    tail = jnp.where(lane < count, wgt_ref[:, 128:160], 0)
    for dst, m, t in (
        (rows, row_ref[:, :128], row_ref[:, 128:160]),
        (slots, smp_ref[:, :128], smp_ref[:, 128:160]),
        (weights, main, tail),
    ):
        dst[0:64, :] = m.astype(F32)
        t = t.astype(F32)
        for k in range(2):
            parts = [t[(4 * k + z) * 8 : (4 * k + z + 1) * 8, :] for z in range(4)]
            dst[64 + 8 * k : 72 + 8 * k, :] = jnp.concatenate(parts, axis=1)


def high_low(r, L):
    h = jnp.floor(r * (1.0 / L))
    return h, r - h * L


def lookup(s, L, rows, slots, weights, t2, oh, xs, put):
    iota = lax.broadcasted_iota(jnp.int32, (256, 128), 0).astype(F32).astype(BF)
    high = []
    for t in range(10):
        h, low = high_low(rows[pl.ds(t * 8 + s, 1), :], L)
        high.append(h)
        for k in range(L // 256):
            key = (low - 256.0 * k).astype(BF)
            oh[k * 256 : (k + 1) * 256, t * 128 : (t + 1) * 128] = jnp.where(iota == key, one(), zero())
    x2 = jnp.dot(t2[...], oh[...], preferred_element_type=F32)
    for t in range(10):
        cols = slice(t * 128, (t + 1) * 128)
        x = x2[0:64, cols]
        for h in range(1, H):
            x = jnp.where(high[t] == float(h), x2[h * 64 : (h + 1) * 64, cols], x)
        x = x.astype(BF)
        if t < 8:
            xs[:, t * 256 : t * 256 + 128] = x
        else:
            for z in range((t - 8) * 4, (t - 8) * 4 + 4):
                xs[:, z * 256 + 128 : z * 256 + 256] = x
    sample = lax.broadcasted_iota(jnp.int32, (128, 128), 0).astype(F32).astype(BF)
    lane = lax.broadcasted_iota(jnp.int32, (1, 128), 1)
    for z in range(8):
        at, tail = z * 8 + s, (8 + z // 4) * 8 + s
        mine = (lane >= 32 * (z % 4)) & (lane < 32 * (z % 4) + 32)
        tail_w = jnp.where(mine, weights[pl.ds(tail, 1), :], 0.0).astype(BF)
        spread = jnp.concatenate(
            [
                jnp.where(sample == slots[pl.ds(at, 1), :].astype(BF), weights[pl.ds(at, 1), :].astype(BF), zero()),
                jnp.where(sample == slots[pl.ds(tail, 1), :].astype(BF), tail_w, zero()),
            ],
            axis=1,
        )
        put(z, lax.dot_general(xs[:, z * 256 : (z + 1) * 256], spread, NT, preferred_element_type=F32))


def gradient(s, L, grad, rows, slots, weights, a, wr, acc):
    iota = lax.broadcasted_iota(jnp.int32, (256, 128), 0).astype(F32).astype(BF)
    lane = lax.broadcasted_iota(jnp.int32, (1, 128), 1)
    for t in range(10):
        cols = slice(t * 128, (t + 1) * 128)
        h, low = high_low(rows[pl.ds(t * 8 + s, 1), :], L)
        h = h.astype(BF)
        w = weights[pl.ds(t * 8 + s, 1), :].astype(BF)
        for k in range(L // 256):
            key = (low - 256.0 * k).astype(BF)
            wr[k * 256 : (k + 1) * 256, cols] = jnp.where(iota == key, w, zero())
        index = jnp.broadcast_to(slots[pl.ds(t * 8 + s, 1), :].astype(jnp.int32), (64, 128))

        def pick(z):
            return jnp.take_along_axis(grad(z).astype(F32), index, axis=1, mode="promise_in_bounds")

        if t < 8:
            e = pick(t)
        else:
            e = pick((t - 8) * 4)
            for z in range(1, 4):
                e = jnp.where(lane >= 32 * z, pick((t - 8) * 4 + z), e)
        e = e.astype(BF)
        for k in range(H):
            a[k * 64 : (k + 1) * 64, cols] = jnp.where(h == jnp.asarray(float(k), BF), e, zero())
    acc[...] += lax.dot_general(a[...], wr[...], NT, preferred_element_type=F32)


def pack(values, dst):
    n, dim, own = values.shape
    row = lax.broadcasted_iota(jnp.int32, (16, own), 0)
    exponents = jnp.zeros((16, own), F32)
    for j in range(n):
        top = jnp.max(jnp.abs(values[j]), axis=0, keepdims=True)
        e = jnp.ceil(jnp.log2(jnp.maximum(top, 1e-30)))
        dst[j * dim : (j + 1) * dim, :] = jnp.round(values[j] * jnp.exp2(14.0 - e)).astype(jnp.int32).astype(jnp.int16)
        exponents = jnp.where(row == j, e, exponents)
    dst[n * dim : n * dim + 16, :] = exponents.astype(jnp.int32).astype(jnp.int16)


def unpack(src, n):
    dim = (src.shape[0] - 16) // n
    exponents = src[n * dim : n * dim + 16, :].astype(jnp.int32).astype(F32)
    return [
        src[j * dim : (j + 1) * dim, :].astype(jnp.int32).astype(F32) * jnp.exp2(exponents[j : j + 1, :] - 14.0)
        for j in range(n)
    ]


def kernel(
    tab_in, accum_in, g, smp_in, row_in, wgt_in, cnt_in,
    pooled_out, new_tab_out, new_accum_out,
    pooled, new_tab, new_accum, store, rows, slots, weights, t2, oh, xs, a, acc,
    gall, part, from_core, two_out, two_in, one_out, one_in, z_out, z_in, squares,
    tab, accum, smp, row, wgt, cnt, load, gz_s, gz_r, gy_s, gy_r, gc_s, gc_r, pc_s, pc_r, py_s, py_r, pz_s, pz_r, sx_s, sx_r,
):
    L = tab.shape[1] // H
    pairs = ((cnt_in, cnt), (wgt_in, wgt), (row_in, row), (smp_in, smp), (tab_in, tab), (accum_in, accum))
    loads = [pltpu.make_async_copy(src, dst, load.at[i]) for i, (src, dst) in enumerate(pairs)]
    r, x = lax.axis_index("rows"), lax.axis_index("dims")
    z, y, c = r // (Y * C), lax.rem(r // C, Y), lax.rem(r, C)

    own_grad = pltpu.make_async_copy(g, gall.at[c, y, z], load.at[len(pairs)])
    own_grad.start()
    for each in loads:
        each.start()

    def z_at(d):
        return (lax.rem(z + d, Z) * (Y * C) + y * C + c, x)

    def y_at(d):
        return (z * (Y * C) + lax.rem(y + d, Y) * C + c, x)

    def x_at(d):
        return (r, lax.rem(x + d, X))

    sibling = (z * (Y * C) + y * C + (1 - c), x)

    def copy(src, dst, send, recv, to):
        return pltpu.make_async_remote_copy(
            src_ref=src, dst_ref=dst, send_sem=send, recv_sem=recv, device_id=to, device_id_type=MESH
        )

    barrier = pltpu.get_barrier_semaphore()
    peers = [z_at(d) for d in range(1, Z)] + [y_at(d) for d in range(1, Y)] + [sibling]
    peers += [x_at(d) for d in range(1, X)]
    for to in peers:
        pl.semaphore_signal(barrier, inc=1, device_id=to, device_id_type=MESH)

    acc[...] = jnp.zeros_like(acc)
    own_grad.wait()
    pl.semaphore_wait(barrier, len(peers))

    along_z = [
        copy(gall.at[c, y, z], gall.at[c, y, z], gz_s.at[d - 1], gz_r.at[d - 1], z_at(d)) for d in range(1, Z)
    ]

    def block_at(d):
        return lax.rem(y + d, Y)

    half = (pl.ds(0, Z // 2), pl.ds(Z // 2, Z // 2))
    def along_y(e):
        at = lax.rem(z + e, Z)
        return [
            copy(gall.at[c, y, at], gall.at[c, y, at], gy_s.at[1 + n, e], gy_r.at[1 + n, e], y_at((1, 3)[n]))
            for n in range(2)
        ]

    near, far = (0, 1, 7), (2, 3, 4, 5, 6)
    def further(e):
        at = lax.rem(z + e, Z)
        up = e in (0, 1, 6, 3)
        block = block_at(3 if up else 1)
        return copy(gall.at[c, block, at], gall.at[c, block, at], gy_s.at[0, e], gy_r.at[0, e], y_at(1 if up else 3))

    def to_core(k):
        block = block_at((0, 1, 3, 2)[k])
        return copy(gall.at[c, block], gall.at[c, block], gc_s.at[k], gc_r.at[k], sibling)

    for each in along_z:
        each.start()

    for each in loads:
        each.wait()
    lay_out(row, smp, wgt, cnt, rows, slots, weights)
    for h in range(H):
        t2[h * 64 : (h + 1) * 64, :] = tab[:, h * L : (h + 1) * L]

    def order(q):
        return block_at(jnp.where(q < 2, 2 - q, jnp.where(q == 2, 3, 0)))

    def to_sibling(q):
        block = order(q)
        return copy(part.at[1 - c, block], from_core.at[q], pc_s.at[q], pc_r.at[q], sibling)

    two_on = [
        copy(two_out.at[0], two_in.at[0], py_s.at[0], py_r.at[0], y_at(2)),
        copy(two_out.at[1], two_in.at[1], py_s.at[1], py_r.at[1], y_at(3)),
    ]
    one_on = [copy(one_out.at[n], one_in.at[n], py_s.at[2 + n], py_r.at[2 + n], y_at((1, 3)[n])) for n in range(2)]

    def add(block, n, packed):
        values = unpack(packed, Z // 2)
        for j in range(Z // 2):
            part[c, block, n * (Z // 2) + j] += values[j]

    def to_z(d):
        return copy(z_out.at[d - 1], z_in.at[d - 1], pz_s.at[d - 1], pz_r.at[d - 1], z_at(d))

    def look(q, side, n):
        block = order(q)

        def put(k, value):
            part[side, block, k] = value

        lookup(block * C + side, L, rows, slots, weights, t2, oh.at[n], xs.at[n], put)

    def add_core(q):
        to_sibling(q).wait_recv()
        part[c, order(q)] += from_core[q]

    look(0, 1 - c, 0)
    to_sibling(0).start()

    @pl.loop(0, Y - 1)
    def _(q):
        look(q, c, 1)
        look(q + 1, 1 - c, 0)
        to_sibling(q + 1).start()
        add_core(q)

        @pl.when(q == 0)
        def _():
            for e in near:
                if e > 0:
                    along_z[Z - e - 1].wait_recv()
                for each in along_y(e):
                    each.start()
            for n in (1, 0):
                pack(part[c, block_at(2), half[n]], two_out.at[n])
                two_on[n].start()

        @pl.when(q == 1)
        def _():
            for e in far:
                along_z[Z - e - 1].wait_recv()
                for each in along_y(e):
                    each.start()
            for m in range(2):
                pack(part[c, block_at(1), half[m]], one_out.at[0, m])
            one_on[0].start()
            to_core(0).start()

        @pl.when(q == 2)
        def _():
            for e in near:
                for each in along_y(e):
                    each.wait_recv()
                further(e).start()
            two_on[1].wait_recv()
            add(block_at(3), 1, two_in.at[1])
            for m in range(2):
                pack(part[c, block_at(3), half[m]], one_out.at[1, m])
            one_on[1].start()

    def grad_of(side, d, n):
        block = block_at(d)

        def grad(k):
            return gall[side, block, k]

        gradient(block * C + side, L, grad, rows, slots, weights, a.at[n], oh.at[n], acc)

    look(Y - 1, c, 1)
    grad_of(c, 0, 0)
    for e in far:
        for each in along_y(e):
            each.wait_recv()
        further(e).start()
    to_core(1).start()
    to_core(2).start()
    add_core(Y - 1)
    to_core(0).wait_recv()

    @pl.loop(0, Y - 1)
    def _(i):

        @pl.when(i == 1)
        def _():
            to_core(1).wait_recv()

        @pl.when(i == 2)
        def _():
            for e in range(Z):
                further(e).wait_recv()
            to_core(3).start()
            to_core(2).wait_recv()

        grad_of(jnp.where(i == 1, c, 1 - c), jnp.where(i == 0, 0, 3), 0)
        grad_of(jnp.where(i == 1, 1 - c, c), jnp.where(i == 2, 2, 1), 1)

        @pl.when(i == 1)
        def _():
            two_on[0].wait_recv()
            add(y, 0, two_in.at[0])
            for n in range(2):
                one_on[n].wait_recv()
                for m in range(2):
                    add(y, m, one_in.at[n, m])
            for d in range(1, Z):
                pack(part[c, y, pl.ds(lax.rem(z + d, Z), 1)], z_out.at[d - 1])
                to_z(d).start()

    to_core(3).wait_recv()
    grad_of(1 - c, 2, 0)

    for h in range(H):
        v = acc[h * 64 : (h + 1) * 64, :]
        squares[x, h : h + 1, :] = jnp.sum(v * v, axis=0, keepdims=True)
    along_x = [
        copy(squares.at[x], squares.at[x], sx_s.at[d - 1], sx_r.at[d - 1], x_at(d)) for d in range(1, X)
    ]
    for each in along_x:
        each.start()

    for d in range(1, Z):
        to_z(d).wait_recv()
    total = part[c, y, z]
    for d in range(1, Z):
        total += unpack(z_in.at[d - 1], 1)[0]
    pooled[...] = total
    out = [pltpu.make_async_copy(pooled, pooled_out, store.at[0])]
    out[0].start()

    for each in along_x:
        each.wait_recv()
    norm = (squares[0] + squares[1]) + (squares[2] + squares[3])
    for h in range(H):
        cols = slice(h * L, (h + 1) * L)
        new = accum[:, cols] + norm[h : h + 1, :] / D
        new_accum[:, cols] = new
        moved = acc[h * 64 : (h + 1) * 64, :] * (STEP * lax.rsqrt(new))
        new_tab[:, cols] = (tab[:, cols].astype(F32) - moved).astype(BF)
        if h % 2 == 1:
            cols = pl.ds((h - 1) * L, 2 * L)
            out.append(pltpu.make_async_copy(new_tab.at[:, cols], new_tab_out.at[:, cols], store.at[2 + h // 2]))
            out[-1].start()
    out.append(pltpu.make_async_copy(new_accum, new_accum_out, store.at[1]))
    out[-1].start()

    for each in along_z + two_on + one_on + along_x:
        each.wait_send()
    for e in range(Z):
        further(e).wait_send()
        for each in along_y(e):
            each.wait_send()
    for q in range(Y):
        to_core(q).wait_send()
        to_sibling(q).wait_send()
    for d in range(1, Z):
        to_z(d).wait_send()
    for each in out:
        each.wait()


def hand_on(*refs):
    n = (len(refs) - 2) // 3
    src, dst, held, come, go = refs[:n], refs[n : 2 * n], refs[2 * n : 3 * n], refs[-2], refs[-1]
    pieces = [(src[1].at[rows], held[1].at[rows], dst[1].at[rows]) for rows in [pl.ds(16 * k, 16) for k in range(4)]]
    pieces += [(src[i], held[i], dst[i]) for i in (0, 2)]
    loads = [pltpu.make_async_copy(p[0], p[1], come.at[i]) for i, p in enumerate(pieces)]
    stores = [pltpu.make_async_copy(p[1], p[2], go.at[i]) for i, p in enumerate(pieces)]
    for each in loads:
        each.start()
    for load, store in zip(loads, stores):
        load.wait()
        store.start()
    for each in stores:
        each.wait()


def shards(table, accum, grad_pooled, sample_slot, row_slot, weight, send_count):
    _, dim, n_rows = table.shape
    own = grad_pooled.shape[2]
    L = n_rows // H
    half_rows = (Z // 2) * dim + 16
    dma = pltpu.SemaphoreType.DMA
    anywhere = pl.BlockSpec(memory_space=pl.ANY)
    shapes = (
        jax.ShapeDtypeStruct((dim, own), F32),
        jax.ShapeDtypeStruct((dim, n_rows), BF),
        jax.ShapeDtypeStruct((1, n_rows), F32),
    )
    results = pl.pallas_call(
        kernel,
        out_shape=shapes,
        in_specs=[anywhere] * 7,
        out_specs=(anywhere,) * 3,
        scratch_shapes=[pltpu.VMEM(each.shape, each.dtype) for each in shapes]
        + [dma((2 + H // 2,))]
        + [pltpu.VMEM((80, 128), F32)] * 3
        + [
            pltpu.VMEM((64 * H, L), BF),
            pltpu.VMEM((2, L, 1280), BF),
            pltpu.VMEM((2, 64, 2048), BF),
            pltpu.VMEM((2, 64 * H, 1280), BF),
            pltpu.VMEM((64 * H, L), F32),
            pltpu.VMEM((C, Y, Z, dim, own), BF),
            pltpu.VMEM((C, Y, Z, dim, own), F32),
            pltpu.VMEM((Y, Z, dim, own), F32),
            pltpu.VMEM((2, half_rows, own), jnp.int16),
            pltpu.VMEM((2, half_rows, own), jnp.int16),
            pltpu.VMEM((2, 2, half_rows, own), jnp.int16),
            pltpu.VMEM((2, 2, half_rows, own), jnp.int16),
            pltpu.VMEM((Z - 1, dim + 16, own), jnp.int16),
            pltpu.VMEM((Z - 1, dim + 16, own), jnp.int16),
            pltpu.VMEM((X, H, L), F32),
        ]
        + [pltpu.VMEM((dim, n_rows), BF), pltpu.VMEM((1, n_rows), F32)]
        + [pltpu.VMEM(sample_slot.shape[2:], jnp.int32)] * 3
        + [pltpu.VMEM(send_count.shape[1:], jnp.int32)]
        + [dma((n,)) for n in (7, 7, 7)]
        + [dma((3, Z)), dma((3, Z))]
        + [dma((n,)) for n in (4, 4, 4, 4, 4, 4, 7, 7, 3, 3)],
        compiler_params=pltpu.CompilerParams(
            collective_id=0, has_side_effects=True, vmem_limit_bytes=64 << 20
        ),
    )(
        table[0],
        accum,
        grad_pooled[0],
        sample_slot[0, 0],
        row_slot[0, 0],
        weight[0, 0],
        send_count[0],
    )
    pooled, new_table, new_accum = pl.pallas_call(
        hand_on,
        out_shape=shapes,
        in_specs=[anywhere] * 3,
        out_specs=(anywhere,) * 3,
        scratch_shapes=[pltpu.VMEM(each.shape, each.dtype) for each in shapes] + [dma((6,)), dma((6,))],
        compiler_params=pltpu.CompilerParams(vmem_limit_bytes=64 << 20),
    )(*results)
    return pooled[None], new_table[None], new_accum


def solution(mesh):
    return jax.shard_map(
        shards,
        mesh=mesh,
        in_specs=(
            P(None, "dims", "rows"),
            P(None, "rows"),
            P(None, "dims", "rows"),
            P(None, "rows", None, None),
            P(None, "rows", None, None),
            P(None, "rows", None, None),
            P(None, "rows", None),
        ),
        out_specs=(P(None, "dims", "rows"), P(None, "dims", "rows"), P(None, "rows")),
        check_vma=False,
    )
```

```python
import jax
import jax.numpy as jnp
from jax import lax
from jax.experimental import pallas as pl
from jax.experimental.pallas import tpu as pltpu
from jax.sharding import PartitionSpec as P

D = 256
STEP = 0.3
H = 8
F32 = jnp.float32
BF = jnp.bfloat16
NT = (((1,), (1,)), ((), ()))
MESH = pl.DeviceIdType.MESH
Z, Y, C, X = 8, 4, 2, 4


def one():
    return jnp.ones((), BF)


def zero():
    return jnp.zeros((), BF)


def lay_out(row_ref, smp_ref, wgt_ref, cnt_ref, rows, slots, weights):
    eye = lax.broadcasted_iota(jnp.int32, (64, 64), 0) == lax.broadcasted_iota(jnp.int32, (64, 64), 1)
    count = jnp.where(eye, jnp.broadcast_to(cnt_ref[...], (64, 64)), 0).astype(F32)
    count = jnp.sum(count, axis=1, keepdims=True).astype(jnp.int32)
    lane = lax.broadcasted_iota(jnp.int32, (64, 128), 1)
    main = jnp.where(lane < count, wgt_ref[:, :128], 0)
    lane = lax.broadcasted_iota(jnp.int32, (64, 32), 1) + 128
    tail = jnp.where(lane < count, wgt_ref[:, 128:160], 0)
    for dst, m, t in (
        (rows, row_ref[:, :128], row_ref[:, 128:160]),
        (slots, smp_ref[:, :128], smp_ref[:, 128:160]),
        (weights, main, tail),
    ):
        dst[0:64, :] = m.astype(F32)
        t = t.astype(F32)
        for k in range(2):
            parts = [t[(4 * k + z) * 8 : (4 * k + z + 1) * 8, :] for z in range(4)]
            dst[64 + 8 * k : 72 + 8 * k, :] = jnp.concatenate(parts, axis=1)


def high_low(r, L):
    h = jnp.floor(r * (1.0 / L))
    return h, r - h * L


def lookup(s, L, rows, slots, weights, t2, oh, xs, put):
    iota = lax.broadcasted_iota(jnp.int32, (256, 128), 0).astype(F32).astype(BF)
    high = []
    for t in range(10):
        h, low = high_low(rows[pl.ds(t * 8 + s, 1), :], L)
        high.append(h)
        for k in range(L // 256):
            key = (low - 256.0 * k).astype(BF)
            oh[k * 256 : (k + 1) * 256, t * 128 : (t + 1) * 128] = jnp.where(iota == key, one(), zero())
    x2 = jnp.dot(t2[...], oh[...], preferred_element_type=F32)
    for t in range(10):
        cols = slice(t * 128, (t + 1) * 128)
        x = x2[0:64, cols]
        for h in range(1, H):
            x = jnp.where(high[t] == float(h), x2[h * 64 : (h + 1) * 64, cols], x)
        x = x.astype(BF)
        if t < 8:
            xs[:, t * 256 : t * 256 + 128] = x
        else:
            for z in range((t - 8) * 4, (t - 8) * 4 + 4):
                xs[:, z * 256 + 128 : z * 256 + 256] = x
    sample = lax.broadcasted_iota(jnp.int32, (128, 128), 0).astype(F32).astype(BF)
    lane = lax.broadcasted_iota(jnp.int32, (1, 128), 1)
    for z in range(8):
        at, tail = z * 8 + s, (8 + z // 4) * 8 + s
        mine = (lane >= 32 * (z % 4)) & (lane < 32 * (z % 4) + 32)
        tail_w = jnp.where(mine, weights[pl.ds(tail, 1), :], 0.0).astype(BF)
        spread = jnp.concatenate(
            [
                jnp.where(sample == slots[pl.ds(at, 1), :].astype(BF), weights[pl.ds(at, 1), :].astype(BF), zero()),
                jnp.where(sample == slots[pl.ds(tail, 1), :].astype(BF), tail_w, zero()),
            ],
            axis=1,
        )
        put(z, lax.dot_general(xs[:, z * 256 : (z + 1) * 256], spread, NT, preferred_element_type=F32))


def gradient(s, L, grad, rows, slots, weights, a, wr, acc):
    iota = lax.broadcasted_iota(jnp.int32, (256, 128), 0).astype(F32).astype(BF)
    lane = lax.broadcasted_iota(jnp.int32, (1, 128), 1)
    for t in range(10):
        cols = slice(t * 128, (t + 1) * 128)
        h, low = high_low(rows[pl.ds(t * 8 + s, 1), :], L)
        h = h.astype(BF)
        w = weights[pl.ds(t * 8 + s, 1), :].astype(BF)
        for k in range(L // 256):
            key = (low - 256.0 * k).astype(BF)
            wr[k * 256 : (k + 1) * 256, cols] = jnp.where(iota == key, w, zero())
        index = jnp.broadcast_to(slots[pl.ds(t * 8 + s, 1), :].astype(jnp.int32), (64, 128))

        def pick(z):
            return jnp.take_along_axis(grad(z).astype(F32), index, axis=1, mode="promise_in_bounds")

        if t < 8:
            e = pick(t)
        else:
            e = pick((t - 8) * 4)
            for z in range(1, 4):
                e = jnp.where(lane >= 32 * z, pick((t - 8) * 4 + z), e)
        e = e.astype(BF)
        for k in range(H):
            a[k * 64 : (k + 1) * 64, cols] = jnp.where(h == jnp.asarray(float(k), BF), e, zero())
    acc[...] += lax.dot_general(a[...], wr[...], NT, preferred_element_type=F32)


def pack(values, dst):
    n, dim, own = values.shape
    row = lax.broadcasted_iota(jnp.int32, (16, own), 0)
    exponents = jnp.zeros((16, own), F32)
    for j in range(n):
        top = jnp.max(jnp.abs(values[j]), axis=0, keepdims=True)
        e = jnp.ceil(jnp.log2(jnp.maximum(top, 1e-30)))
        dst[j * dim : (j + 1) * dim, :] = jnp.round(values[j] * jnp.exp2(14.0 - e)).astype(jnp.int32).astype(jnp.int16)
        exponents = jnp.where(row == j, e, exponents)
    dst[n * dim : n * dim + 16, :] = exponents.astype(jnp.int32).astype(jnp.int16)


def unpack(src, n):
    dim = (src.shape[0] - 16) // n
    exponents = src[n * dim : n * dim + 16, :].astype(jnp.int32).astype(F32)
    return [
        src[j * dim : (j + 1) * dim, :].astype(jnp.int32).astype(F32) * jnp.exp2(exponents[j : j + 1, :] - 14.0)
        for j in range(n)
    ]


def kernel(
    tab_in, accum_in, g, smp_in, row_in, wgt_in, cnt_in,
    pooled_out, new_tab_out, new_accum_out,
    pooled, new_tab, new_accum, store, rows, slots, weights, t2, oh, xs, a, acc,
    gall, part, from_core, two_out, two_in, one_out, one_in, z_out, z_in, squares,
    tab, accum, smp, row, wgt, cnt, load, gz_s, gz_r, gy_s, gy_r, gc_s, gc_r, pc_s, pc_r, py_s, py_r, pz_s, pz_r, sx_s, sx_r,
):
    L = tab.shape[1] // H
    pairs = ((cnt_in, cnt), (wgt_in, wgt), (row_in, row), (smp_in, smp), (tab_in, tab), (accum_in, accum))
    loads = [pltpu.make_async_copy(src, dst, load.at[i]) for i, (src, dst) in enumerate(pairs)]
    r, x = lax.axis_index("rows"), lax.axis_index("dims")
    z, y, c = r // (Y * C), lax.rem(r // C, Y), lax.rem(r, C)

    own_grad = pltpu.make_async_copy(g, gall.at[c, y, z], load.at[len(pairs)])
    own_grad.start()
    for each in loads:
        each.start()

    def z_at(d):
        return (lax.rem(z + d, Z) * (Y * C) + y * C + c, x)

    def y_at(d):
        return (z * (Y * C) + lax.rem(y + d, Y) * C + c, x)

    def x_at(d):
        return (r, lax.rem(x + d, X))

    sibling = (z * (Y * C) + y * C + (1 - c), x)

    def copy(src, dst, send, recv, to):
        return pltpu.make_async_remote_copy(
            src_ref=src, dst_ref=dst, send_sem=send, recv_sem=recv, device_id=to, device_id_type=MESH
        )

    barrier = pltpu.get_barrier_semaphore()
    peers = [z_at(d) for d in range(1, Z)] + [y_at(d) for d in range(1, Y)] + [sibling]
    peers += [x_at(d) for d in range(1, X)]
    for to in peers:
        pl.semaphore_signal(barrier, inc=1, device_id=to, device_id_type=MESH)

    acc[...] = jnp.zeros_like(acc)
    pl.semaphore_wait(barrier, len(peers))

    along_z = [
        copy(g, gall.at[c, y, z], gz_s.at[d - 1], gz_r.at[d - 1], z_at(d)) for d in range(1, Z)
    ]

    def block_at(d):
        return lax.rem(y + d, Y)

    half = (pl.ds(0, Z // 2), pl.ds(Z // 2, Z // 2))
    def along_y(e):
        at = lax.rem(z + e, Z)
        return [
            copy(gall.at[c, y, at], gall.at[c, y, at], gy_s.at[1 + n, e], gy_r.at[1 + n, e], y_at((1, 3)[n]))
            for n in range(2)
        ]

    near, far = (0, 1, 7), (2, 3, 4, 5, 6)
    def further(e):
        at = lax.rem(z + e, Z)
        up = e in (0, 1, 6, 3)
        block = block_at(3 if up else 1)
        return copy(gall.at[c, block, at], gall.at[c, block, at], gy_s.at[0, e], gy_r.at[0, e], y_at(1 if up else 3))

    def to_core(k):
        block = block_at((0, 1, 3, 2)[k])
        return copy(gall.at[c, block], gall.at[c, block], gc_s.at[k], gc_r.at[k], sibling)

    for each in along_z:
        each.start()

    for each in [own_grad] + loads:
        each.wait()
    lay_out(row, smp, wgt, cnt, rows, slots, weights)
    for h in range(H):
        t2[h * 64 : (h + 1) * 64, :] = tab[:, h * L : (h + 1) * L]

    def order(q):
        return block_at(jnp.where(q < 2, 2 - q, jnp.where(q == 2, 3, 0)))

    def to_sibling(q):
        block = order(q)
        return copy(part.at[1 - c, block], from_core.at[q], pc_s.at[q], pc_r.at[q], sibling)

    two_on = [
        copy(two_out.at[0], two_in.at[0], py_s.at[0], py_r.at[0], y_at(2)),
        copy(two_out.at[1], two_in.at[1], py_s.at[1], py_r.at[1], y_at(3)),
    ]
    one_on = [copy(one_out.at[n], one_in.at[n], py_s.at[2 + n], py_r.at[2 + n], y_at((1, 3)[n])) for n in range(2)]

    def add(block, n, packed):
        values = unpack(packed, Z // 2)
        for j in range(Z // 2):
            part[c, block, n * (Z // 2) + j] += values[j]

    def to_z(d):
        return copy(z_out.at[d - 1], z_in.at[d - 1], pz_s.at[d - 1], pz_r.at[d - 1], z_at(d))

    def look(q, side, n):
        block = order(q)

        def put(k, value):
            part[side, block, k] = value

        lookup(block * C + side, L, rows, slots, weights, t2, oh.at[n], xs.at[n], put)

    def add_core(q):
        to_sibling(q).wait_recv()
        part[c, order(q)] += from_core[q]

    look(0, 1 - c, 0)
    to_sibling(0).start()

    @pl.loop(0, Y - 1)
    def _(q):
        look(q, c, 1)
        look(q + 1, 1 - c, 0)
        to_sibling(q + 1).start()
        add_core(q)

        @pl.when(q == 0)
        def _():
            for e in near:
                if e > 0:
                    along_z[Z - e - 1].wait_recv()
                for each in along_y(e):
                    each.start()
            for n in (1, 0):
                pack(part[c, block_at(2), half[n]], two_out.at[n])
                two_on[n].start()

        @pl.when(q == 1)
        def _():
            for e in far:
                along_z[Z - e - 1].wait_recv()
                for each in along_y(e):
                    each.start()
            for m in range(2):
                pack(part[c, block_at(1), half[m]], one_out.at[0, m])
            one_on[0].start()
            to_core(0).start()

        @pl.when(q == 2)
        def _():
            for e in near:
                for each in along_y(e):
                    each.wait_recv()
                further(e).start()
            two_on[1].wait_recv()
            add(block_at(3), 1, two_in.at[1])
            for m in range(2):
                pack(part[c, block_at(3), half[m]], one_out.at[1, m])
            one_on[1].start()

    def grad_of(side, d, n):
        block = block_at(d)

        def grad(k):
            return gall[side, block, k]

        gradient(block * C + side, L, grad, rows, slots, weights, a.at[n], oh.at[n], acc)

    look(Y - 1, c, 1)
    grad_of(c, 0, 0)
    for e in far:
        for each in along_y(e):
            each.wait_recv()
        further(e).start()
    to_core(1).start()
    to_core(2).start()
    add_core(Y - 1)
    to_core(0).wait_recv()

    @pl.loop(0, Y - 1)
    def _(i):

        @pl.when(i == 1)
        def _():
            to_core(1).wait_recv()

        @pl.when(i == 2)
        def _():
            for e in range(Z):
                further(e).wait_recv()
            to_core(3).start()
            to_core(2).wait_recv()

        grad_of(jnp.where(i == 1, c, 1 - c), jnp.where(i == 0, 0, 3), 0)
        grad_of(jnp.where(i == 1, 1 - c, c), jnp.where(i == 2, 2, 1), 1)

        @pl.when(i == 1)
        def _():
            two_on[0].wait_recv()
            add(y, 0, two_in.at[0])
            for n in range(2):
                one_on[n].wait_recv()
                for m in range(2):
                    add(y, m, one_in.at[n, m])
            for d in range(1, Z):
                pack(part[c, y, pl.ds(lax.rem(z + d, Z), 1)], z_out.at[d - 1])
                to_z(d).start()

    to_core(3).wait_recv()
    grad_of(1 - c, 2, 0)

    for h in range(H):
        v = acc[h * 64 : (h + 1) * 64, :]
        squares[x, h : h + 1, :] = jnp.sum(v * v, axis=0, keepdims=True)
    along_x = [
        copy(squares.at[x], squares.at[x], sx_s.at[d - 1], sx_r.at[d - 1], x_at(d)) for d in range(1, X)
    ]
    for each in along_x:
        each.start()

    for d in range(1, Z):
        to_z(d).wait_recv()
    total = part[c, y, z]
    for d in range(1, Z):
        total += unpack(z_in.at[d - 1], 1)[0]
    pooled[...] = total
    out = [pltpu.make_async_copy(pooled, pooled_out, store.at[0])]
    out[0].start()

    for each in along_x:
        each.wait_recv()
    norm = (squares[0] + squares[1]) + (squares[2] + squares[3])
    for h in range(H):
        cols = slice(h * L, (h + 1) * L)
        new = accum[:, cols] + norm[h : h + 1, :] / D
        new_accum[:, cols] = new
        moved = acc[h * 64 : (h + 1) * 64, :] * (STEP * lax.rsqrt(new))
        new_tab[:, cols] = (tab[:, cols].astype(F32) - moved).astype(BF)
        if h % 2 == 1:
            cols = pl.ds((h - 1) * L, 2 * L)
            out.append(pltpu.make_async_copy(new_tab.at[:, cols], new_tab_out.at[:, cols], store.at[2 + h // 2]))
            out[-1].start()
    out.append(pltpu.make_async_copy(new_accum, new_accum_out, store.at[1]))
    out[-1].start()

    for each in along_z + two_on + one_on + along_x:
        each.wait_send()
    for e in range(Z):
        further(e).wait_send()
        for each in along_y(e):
            each.wait_send()
    for q in range(Y):
        to_core(q).wait_send()
        to_sibling(q).wait_send()
    for d in range(1, Z):
        to_z(d).wait_send()
    for each in out:
        each.wait()


def hand_on(*refs):
    n = (len(refs) - 2) // 3
    src, dst, held, come, go = refs[:n], refs[n : 2 * n], refs[2 * n : 3 * n], refs[-2], refs[-1]
    pieces = [(src[1].at[rows], held[1].at[rows], dst[1].at[rows]) for rows in [pl.ds(16 * k, 16) for k in range(4)]]
    pieces += [(src[i], held[i], dst[i]) for i in (0, 2)]
    loads = [pltpu.make_async_copy(p[0], p[1], come.at[i]) for i, p in enumerate(pieces)]
    stores = [pltpu.make_async_copy(p[1], p[2], go.at[i]) for i, p in enumerate(pieces)]
    for each in loads:
        each.start()
    for load, store in zip(loads, stores):
        load.wait()
        store.start()
    for each in stores:
        each.wait()


def shards(table, accum, grad_pooled, sample_slot, row_slot, weight, send_count):
    _, dim, n_rows = table.shape
    own = grad_pooled.shape[2]
    L = n_rows // H
    half_rows = (Z // 2) * dim + 16
    dma = pltpu.SemaphoreType.DMA
    anywhere = pl.BlockSpec(memory_space=pl.ANY)
    shapes = (
        jax.ShapeDtypeStruct((dim, own), F32),
        jax.ShapeDtypeStruct((dim, n_rows), BF),
        jax.ShapeDtypeStruct((1, n_rows), F32),
    )
    results = pl.pallas_call(
        kernel,
        out_shape=shapes,
        in_specs=[anywhere] * 7,
        out_specs=(anywhere,) * 3,
        scratch_shapes=[pltpu.VMEM(each.shape, each.dtype) for each in shapes]
        + [dma((2 + H // 2,))]
        + [pltpu.VMEM((80, 128), F32)] * 3
        + [
            pltpu.VMEM((64 * H, L), BF),
            pltpu.VMEM((2, L, 1280), BF),
            pltpu.VMEM((2, 64, 2048), BF),
            pltpu.VMEM((2, 64 * H, 1280), BF),
            pltpu.VMEM((64 * H, L), F32),
            pltpu.VMEM((C, Y, Z, dim, own), BF),
            pltpu.VMEM((C, Y, Z, dim, own), F32),
            pltpu.VMEM((Y, Z, dim, own), F32),
            pltpu.VMEM((2, half_rows, own), jnp.int16),
            pltpu.VMEM((2, half_rows, own), jnp.int16),
            pltpu.VMEM((2, 2, half_rows, own), jnp.int16),
            pltpu.VMEM((2, 2, half_rows, own), jnp.int16),
            pltpu.VMEM((Z - 1, dim + 16, own), jnp.int16),
            pltpu.VMEM((Z - 1, dim + 16, own), jnp.int16),
            pltpu.VMEM((X, H, L), F32),
        ]
        + [pltpu.VMEM((dim, n_rows), BF), pltpu.VMEM((1, n_rows), F32)]
        + [pltpu.VMEM(sample_slot.shape[2:], jnp.int32)] * 3
        + [pltpu.VMEM(send_count.shape[1:], jnp.int32)]
        + [dma((n,)) for n in (7, 7, 7)]
        + [dma((3, Z)), dma((3, Z))]
        + [dma((n,)) for n in (4, 4, 4, 4, 4, 4, 7, 7, 3, 3)],
        compiler_params=pltpu.CompilerParams(
            collective_id=0, has_side_effects=True, vmem_limit_bytes=64 << 20
        ),
    )(
        table[0],
        accum,
        grad_pooled[0],
        sample_slot[0, 0],
        row_slot[0, 0],
        weight[0, 0],
        send_count[0],
    )
    pooled, new_table, new_accum = pl.pallas_call(
        hand_on,
        out_shape=shapes,
        in_specs=[anywhere] * 3,
        out_specs=(anywhere,) * 3,
        scratch_shapes=[pltpu.VMEM(each.shape, each.dtype) for each in shapes] + [dma((6,)), dma((6,))],
        compiler_params=pltpu.CompilerParams(vmem_limit_bytes=64 << 20),
    )(*results)
    return pooled[None], new_table[None], new_accum


def solution(mesh):
    return jax.shard_map(
        shards,
        mesh=mesh,
        in_specs=(
            P(None, "dims", "rows"),
            P(None, "rows"),
            P(None, "dims", "rows"),
            P(None, "rows", None, None),
            P(None, "rows", None, None),
            P(None, "rows", None, None),
            P(None, "rows", None),
        ),
        out_specs=(P(None, "dims", "rows"), P(None, "dims", "rows"), P(None, "rows")),
        check_vma=False,
    )
```
